256 devices in a mesh: lon: 16 (over y_hi, x, core), lat: 16 (over z, y_lo).
Axes of the slice: x: 4, y: 4 (y_hi: 2, y_lo: 2; y = y_hi * 2 + y_lo), z: 8, core: 2. Of those that a mesh axis runs over, the one named last changes fastest.
Arguments:
- grid_state: bfloat16 [224, 1024, 256], P('lat', 'lon'), may hold values from -6 to 6
- row_query: bfloat16 [256, 256], replicated, may hold values from -15 to 15
- row_keyval: bfloat16 [256, 512], replicated, may hold values from -0.375 to 0.375
- row_output: bfloat16 [256, 256], replicated, may hold values from -0.375 to 0.375
- column_query: bfloat16 [256, 256], replicated, may hold values from -15 to 15
- column_keyval: bfloat16 [256, 512], replicated, may hold values from -0.375 to 0.375
- column_output: bfloat16 [256, 256], replicated, may hold values from -1 to 1
- conv_kernel: float32 [4, 9, 256], replicated, may hold values from -2 to 2
- gate_up: bfloat16 [256, 2048], replicated, may hold values from -0.375 to 0.375
- down_proj: bfloat16 [1024, 256], replicated, may hold values from -0.1875 to 0.1875
Outputs:
- block_out: bfloat16 [224, 1024, 256], P('lat', 'lon')
The draws below stay inside these ranges and needn't reach their ends.
All inputs are finite; a program needn't handle non-finite values.
Results may differ from the reference program's by a relative error of at most 0.039.
The reference program's roundings to bfloat16 on the way count: a program that leaves them out, or rounds other values in their place, can miss the bound.
Values may be sent and summed in bfloat16 or wider, within the bound.
No kernel may reach another device: no remote copies, remote signals or barrier semaphores. Data moves between devices by JAX's collectives and lax.ppermute only.
A program may use at most 128 MiB of HBM per device.

```python
import jax
import jax.numpy as jnp
from jax import lax

C = 256
HEADS = 8
FF = 1024
LAT = 224
LON = 1024


def head_query(key, width, heads, lowest, highest):
    base = jax.random.truncated_normal(jax.random.fold_in(key, 1), -4.0, 4.0, (width, width), jnp.float32) * width ** (-0.5)
    gains = jnp.exp(jax.random.uniform(jax.random.fold_in(key, 2), (heads,), jnp.float32, jnp.log(lowest), jnp.log(highest)))
    return (base * jnp.repeat(gains, width // heads)[None, :]).astype(jnp.bfloat16)


def draw_row_query(key, part):
    key = jax.random.fold_in(key, 11)
    return head_query(key, C, HEADS, 0.5, 3.0)


def draw_column_query(key, part):
    key = jax.random.fold_in(key, 23)
    return head_query(key, C, HEADS, 0.5, 3.0)


def shard_levels(own_key, shape, split, least, largest):
    gain = 1.0
    for axis_at, parts in split:
        heights = jax.random.uniform(jax.random.fold_in(jax.random.fold_in(own_key, 6), axis_at), (parts,), jnp.float32, least / len(split), largest / len(split))
        gain = gain * jnp.repeat(jnp.exp(heights), shape[axis_at] // parts).reshape((-1,) + (1,) * (len(shape) - 1 - axis_at))
    return gain


def gaussian(key, shape, scale, bound, split=(), kind=jnp.bfloat16):
    values = scale * jax.random.normal(key, shape, jnp.float32)
    if split:
        values = values * shard_levels(key, shape, split, -0.22, 0.18)
    return jnp.clip(values, -bound, bound).astype(kind)


def setup_inputs(seed: int = 0) -> dict:
    key_of = jax.random.split(jax.random.key(seed), 11)
    return {
        "grid_state": gaussian(key_of[0], (LAT, LON, C), 1.0, 6.0, ((0, 16), (1, 16))),
        "row_query": draw_row_query(jax.random.fold_in(key_of[10], 71), 0),
        "row_keyval": gaussian(key_of[2], (C, 2 * C), C ** -0.5, 0.375),
        "row_output": gaussian(key_of[3], (C, C), C ** -0.5, 0.375),
        "column_query": draw_column_query(jax.random.fold_in(key_of[10], 71), 0),
        "column_keyval": gaussian(key_of[5], (C, 2 * C), C ** -0.5, 0.375),
        "column_output": gaussian(key_of[6], (C, C), (C // 8) ** -0.5, 1.0),
        "conv_kernel": gaussian(key_of[7], (4, 9, C), 9 ** -0.5, 2.0, (), jnp.float32),
        "gate_up": gaussian(key_of[8], (C, 2 * FF), C ** -0.5, 0.375),
        "down_proj": gaussian(key_of[9], (FF, C), FF ** -0.5, 0.1875),
    }


def normalize(values):
    floats = values.astype(jnp.float32)
    center = floats - lax.optimization_barrier(jnp.mean(floats, axis=-1, keepdims=True))
    spread = lax.optimization_barrier(jnp.mean(center * center, axis=-1, keepdims=True))
    return (center * lax.rsqrt(spread + 1e-05)).astype(jnp.bfloat16)

def project(normed, weight):
    flat = normed.reshape(-1, normed.shape[-1])
    result = jnp.dot(flat, weight, preferred_element_type=jnp.float32).astype(jnp.bfloat16)
    return result.reshape(normed.shape[:-1] + (weight.shape[1],))

def attend(items):
    queries, keyvals = items
    width = queries.shape[-1]
    head_size = width // HEADS
    qheads = queries.astype(jnp.float32).reshape(-1, HEADS, head_size)
    keys = keyvals[:, :width].astype(jnp.float32).reshape(-1, HEADS, head_size)
    values = keyvals[:, width:].astype(jnp.float32).reshape(-1, HEADS, head_size)
    scores = jnp.einsum('qhd,khd->hqk', qheads, keys) * head_size ** (-0.5)
    highest = lax.optimization_barrier(jnp.max(scores, axis=-1, keepdims=True))
    weights = jnp.exp(scores - highest).astype(jnp.bfloat16).astype(jnp.float32)
    totals = lax.optimization_barrier(jnp.sum(weights, axis=-1))
    mixed = jnp.einsum('hqk,khd->qhd', weights, values) / jnp.transpose(totals)[:, :, None]
    return mixed.reshape(-1, width).astype(jnp.bfloat16)

def attention_layer(state, query_weight, keyval_weight, output_weight, columns):
    normed = normalize(state)
    queries = project(normed, query_weight)
    keyvals = project(normed, keyval_weight)
    if columns:
        queries = jnp.swapaxes(queries, 0, 1)
        keyvals = jnp.swapaxes(keyvals, 0, 1)
    mixed = lax.map(attend, (queries, keyvals))
    if columns:
        mixed = jnp.swapaxes(mixed, 0, 1)
    width = state.shape[-1]
    update = jnp.dot(mixed.reshape(-1, width), output_weight, preferred_element_type=jnp.float32)
    return (state.astype(jnp.float32) + update.reshape(state.shape)).astype(jnp.bfloat16)

def reference(grid_state, row_query, row_keyval, row_output, column_query, column_keyval, column_output, conv_kernel, gate_up, down_proj):
    after_rows = attention_layer(grid_state, row_query, row_keyval, row_output, False)
    state = attention_layer(after_rows, column_query, column_keyval, column_output, True)
    height = state.shape[0]
    breadth = state.shape[1]
    for level in range(4):
        dilation = 2 ** level
        floats = state.astype(jnp.float32)
        wrapped = jnp.concatenate([floats[:, breadth - dilation:], floats, floats[:, :dilation]], axis=1)
        padded = jnp.pad(wrapped, ((dilation, dilation), (0, 0), (0, 0)))
        total = jnp.zeros_like(floats)
        for tap in range(9):
            row_off = tap // 3 * dilation
            col_off = tap % 3 * dilation
            total = total + conv_kernel[level, tap] * padded[row_off:row_off + height, col_off:col_off + breadth]
        state = (floats + jax.nn.gelu(total, approximate=False)).astype(jnp.bfloat16)
    normed = normalize(state).reshape(-1, state.shape[-1])
    both = jnp.dot(normed, gate_up, preferred_element_type=jnp.float32)
    hidden_units = gate_up.shape[1] // 2
    hidden = (jax.nn.silu(both[:, :hidden_units]) * both[:, hidden_units:]).astype(jnp.bfloat16)
    update = jnp.dot(hidden, down_proj, preferred_element_type=jnp.float32)
    return (state.astype(jnp.float32) + update.reshape(state.shape)).astype(jnp.bfloat16)
```

```python
import functools
import jax
import jax.numpy as jnp
import numpy as np
from jax import lax
from jax.sharding import PartitionSpec as P
from jax.experimental import pallas as pl
from jax.experimental.pallas import tpu as pltpu

BF = jnp.bfloat16
F32 = jnp.float32
HEADS = 8
NT = (((1,), (1,)), ((), ()))
SCALE = 1.4426950408889634 * 32**-0.5
VMEM = pl.BlockSpec(memory_space=pltpu.VMEM)
LIMIT = 56 * 2**20


def norm(values):
    values = values.astype(F32)
    center = values - jnp.mean(values, -1, keepdims=True)
    spread = jnp.mean(center * center, -1, keepdims=True)
    return (center * lax.rsqrt(spread + 1e-5)).astype(BF)


def mm(a, b):
    return jnp.dot(a, b, preferred_element_type=F32)


def value_blocks(values):
    lane = lax.broadcasted_iota(jnp.int32, (1, 128), 1) >> 5
    one = jnp.ones((values.shape[0], 128), BF)
    for h in range(HEADS):
        group = values[:, 128 * (h // 4) : 128 * (h // 4) + 128]
        yield h, jnp.concatenate([jnp.where(lane == h % 4, group, jnp.zeros_like(group)), one], -1)


def attend(q, keys, value_of):
    lane = lax.broadcasted_iota(jnp.int32, (1, 256), 1) >> 5
    halves = []
    for g in range(2):
        total = None
        for h in range(4 * g, 4 * g + 4):
            masked = jnp.where(lane == h, q, jnp.zeros_like(q))
            scores = lax.dot_general(masked, keys, NT, preferred_element_type=F32)
            highest = jnp.max(scores, -1, keepdims=True)
            weights = jnp.exp2((scores - highest) * SCALE).astype(BF)
            sums = mm(weights, value_of(h))
            part = sums[:, :128] / sums[:, 128:]
            total = part if total is None else total + part
        halves.append(total.astype(BF))
    return jnp.concatenate(halves, -1)


def row_kernel(qb, x_ref, wq_ref, wkv_ref, wo_ref, o_ref, q_s, k_s, v_s):
    rows = x_ref.shape[0]
    n = norm(x_ref[...])
    q_s[...] = mm(n, wq_ref[...]).astype(BF)
    kv = mm(n, wkv_ref[...]).astype(BF)
    k_s[...] = kv[:, :256]
    for h, block in value_blocks(kv[:, 256:]):
        v_s[h] = block

    def body(i, _):
        sl = pl.ds(pl.multiple_of(i * qb, qb), qb)
        mixed = attend(q_s[sl, :], k_s[...], lambda h: v_s[h])
        o_ref[sl, :] = (x_ref[sl, :].astype(F32) + mm(mixed, wo_ref[...])).astype(BF)
        return 0

    lax.fori_loop(0, rows // qb, body, 0)


def row_attention(x, wq, wkv, wo, qb=256):
    rows = x.shape[0]
    return pl.pallas_call(
        functools.partial(row_kernel, qb),
        out_shape=jax.ShapeDtypeStruct((rows, 256), BF),
        in_specs=[VMEM] * 4,
        out_specs=VMEM,
        scratch_shapes=[
            pltpu.VMEM((rows, 256), BF),
            pltpu.VMEM((rows, 256), BF),
            pltpu.VMEM((HEADS, rows, 256), BF),
        ],
        compiler_params=pltpu.CompilerParams(vmem_limit_bytes=LIMIT),
        name="row_attention",
    )(x, wq, wkv, wo)


def column_kernel(x_ref, wq_ref, wkv_ref, wo_ref, sel_ref, o_ref):
    lons, lats, _ = x_ref.shape
    peers, _, span, _ = o_ref.shape

    def body(b, _):
        x = x_ref[b]
        n = norm(x)
        q = mm(n, wq_ref[...]).astype(BF)
        kv = mm(n, wkv_ref[...]).astype(BF)
        blocks = dict(value_blocks(kv[:, 256:]))
        mixed = attend(q, kv[:, :256], lambda h: blocks[h])
        after = (x.astype(F32) + mm(mixed, wo_ref[...])).astype(BF)
        sent = mm(sel_ref[...], after).astype(BF)
        for p in range(peers):
            o_ref[p, b] = sent[p * span : (p + 1) * span]
        return 0

    lax.fori_loop(0, lons, body, 0)


def column_attention(x, wq, wkv, wo, select, peers, span):
    lons, lats, _ = x.shape
    return pl.pallas_call(
        column_kernel,
        out_shape=jax.ShapeDtypeStruct((peers, lons, span, 256), BF),
        in_specs=[VMEM] * 5,
        out_specs=VMEM,
        compiler_params=pltpu.CompilerParams(vmem_limit_bytes=LIMIT),
        name="column_attention",
    )(x, wq, wkv, wo, select)


REACH = 15
T, S, PADT = 12, 8, 8
PHI = (
    0.7978842684056429,
    0.036334149112092734,
    -3.302669371540545e-05,
    -5.527338951263253e-05,
    3.974071180846511e-06,
    -1.3378322665984367e-07,
    1.8139279113192596e-09,
)


def gelu(v):
    square = jnp.minimum(v * v, 40.0)
    p = jnp.full_like(square, PHI[-1])
    for c in PHI[-2::-1]:
        p = p * square + c
    half = 0.5 * v
    return half + half * jnp.tanh(v * p)


def conv_mlp_kernel(first_ref, left_ref, own_ref, right_ref, w_ref, gu_ref, down_ref, o_ref, a_s, b_s, f_s):
    per = own_ref.shape[1]
    lat_rows = o_ref.shape[0]
    rows0 = lat_rows + 2 * REACH
    first = first_ref[0]

    def shift(v, by):
        return pltpu.roll(v, by % S, 0)

    def put(ref, hf, row, t, v, reach):
        ref[hf, row, PADT + t] = v
        if t >= T - reach:
            ref[hf, row, PADT + t - T] = shift(v, 1)
        if t < reach:
            ref[hf, row, PADT + t + T] = shift(v, -1)

    parts = [(left_ref, k) for k in range(left_ref.shape[0])]
    parts += [(own_ref, k) for k in range(own_ref.shape[0])]
    parts += [(right_ref, k) for k in range(right_ref.shape[0])]
    for n, (ref, k) in enumerate(parts):
        for b in range(per):
            lon = n * per + b
            s, t = lon // T, lon % T
            for hf in range(2):
                v = ref[k, b, :rows0, hf * 128 : hf * 128 + 128].astype(F32)
                f_s[t, hf, pl.ds(s, rows0, S), :] = v

    def stage(i, _):
        for hf in range(2):
            for t in range(T):
                v = f_s[t, hf, pl.ds(pl.multiple_of(i * S, S), S), :]
                put(a_s, hf, i, t, v, 1)
        return 0

    lax.fori_loop(0, rows0, stage, 0)

    src, dst = a_s, b_s
    edge = 0
    for level in range(4):
        rate = 2**level
        edge += rate
        count = rows0 - 2 * edge
        for hf in range(2):
            taps = [w_ref[level, k, hf] for k in range(9)]

            def row(i, _, src=src, dst=dst, taps=taps, hf=hf, rate=rate, edge=edge, level=level):
                i = i + edge
                lat = first + i
                inside = jnp.logical_and(lat >= 0, lat < LATS).astype(F32)
                for t in range(T):
                    total = None
                    for a in range(3):
                        for b in range(3):
                            term = taps[3 * a + b] * src[hf, i + (a - 1) * rate, PADT + t + (b - 1) * rate]
                            total = term if total is None else total + term
                    new = src[hf, i, PADT + t] + gelu(total)
                    new = new.astype(BF).astype(F32)
                    if level < 3:
                        put(dst, hf, i, t, new * inside, 2 * rate)
                    else:
                        f_s[0, hf, pl.ds((i - edge) * (S * T) + t, S, T), :] = new
                return 0

            lax.fori_loop(0, count, row, 0)
        src, dst = dst, src

    own_cols = o_ref.shape[1]
    batch = 7

    def feed(c, _):
        cells = []
        for d in range(batch):
            at = pl.multiple_of((c * batch + d) * (S * T) + 2 * S, S)
            cells.append(
                jnp.concatenate([f_s[0, hf, pl.ds(at, own_cols), :] for hf in range(2)], -1)
            )
        state = jnp.concatenate(cells, 0)
        normed = norm(state)
        both = mm(normed, gu_ref[...])
        units = gu_ref.shape[1] // 2
        gate, up = both[:, :units], both[:, units:]
        hidden = (gate / (1.0 + jnp.exp(-gate)) * up).astype(BF)
        out = (state + mm(hidden, down_ref[...])).astype(BF)
        o_ref[pl.ds(c * batch, batch)] = out.reshape(batch, own_cols, 256)
        return 0

    lax.fori_loop(0, lat_rows // batch, feed, 0)


LATS = 224


def conv_mlp(first, left, own, right, taps, gate_up, down, lat_rows, own_cols):
    rows0 = lat_rows + 2 * REACH
    return pl.pallas_call(
        conv_mlp_kernel,
        out_shape=jax.ShapeDtypeStruct((lat_rows, own_cols, 256), BF),
        in_specs=[pl.BlockSpec(memory_space=pltpu.SMEM)] + [VMEM] * 6,
        out_specs=VMEM,
        scratch_shapes=[
            pltpu.VMEM((2, rows0, T + 2 * PADT, S, 128), F32),
            pltpu.VMEM((2, rows0, T + 2 * PADT, S, 128), F32),
            pltpu.VMEM((T, 2, max(rows0 * S, lat_rows * S * T), 128), F32),
        ],
        compiler_params=pltpu.CompilerParams(vmem_limit_bytes=LIMIT),
        name="conv_mlp",
    )(first, left, own, right, taps, gate_up, down)


def selection(lats, rows, span):
    blocks = lats // rows
    pick = np.zeros((blocks * span, lats), np.float32)
    for p in range(blocks):
        for r in range(rows + 2 * REACH):
            lat = p * rows - REACH + r
            if 0 <= lat < lats:
                pick[p * span + r, (lat % rows) * blocks + lat // rows] = 1
    return pick.astype(BF)


def on_device(
    grid_state,
    row_query,
    row_keyval,
    row_output,
    column_query,
    column_keyval,
    column_output,
    conv_kernel,
    gate_up,
    down_proj,
):
    rows, cols, width = grid_state.shape
    n = lax.axis_size("lon")
    m = lax.axis_size("lat")
    lons = cols // m
    span = 48
    padded = jnp.pad(grid_state, ((0, n - rows), (0, 0), (0, 0)))
    lines = lax.all_to_all(padded, "lon", 0, 0, tiled=True).reshape(n * cols, width)
    after_rows = row_attention(lines, row_query, row_keyval, row_output)
    moved = lax.all_to_all(after_rows.reshape(n * m, lons, width), ("lon", "lat"), 0, 0, tiled=True)
    moved = jnp.swapaxes(moved[: rows * m], 0, 1)
    pick = jnp.asarray(selection(rows * m, rows, span))
    sent = column_attention(moved, column_query, column_keyval, column_output, pick, m, span)
    own = lax.all_to_all(sent.reshape(m, lons * span, width), "lat", 0, 0, tiled=True)
    own = own.reshape(m, lons, span, width)
    k = 16 // lons
    left = lax.ppermute(own[m - k :], "lon", [(i, (i + 1) % n) for i in range(n)])
    right = lax.ppermute(own[:k], "lon", [((i + 1) % n, i) for i in range(n)])
    first = (lax.axis_index("lat") * rows - REACH).astype(jnp.int32).reshape(1)
    taps = jnp.broadcast_to(conv_kernel.reshape(4, 9, 2, 1, 128), (4, 9, 2, 8, 128))
    return conv_mlp(first, left, own, right, taps, gate_up, down_proj, rows, cols)


def solution(mesh):
    return jax.shard_map(
        on_device,
        mesh=mesh,
        in_specs=(P("lat", "lon", None), P(), P(), P(), P(), P(), P(), P(), P(), P()),
        out_specs=P("lat", "lon", None),
        check_vma=False,
    )
```

```python
import functools
import jax
import jax.numpy as jnp
import numpy as np
from jax import lax
from jax.sharding import PartitionSpec as P
from jax.experimental import pallas as pl
from jax.experimental.pallas import tpu as pltpu

BF = jnp.bfloat16
F32 = jnp.float32
HEADS = 8
NT = (((1,), (1,)), ((), ()))
SCALE = 1.4426950408889634 * 32**-0.5
VMEM = pl.BlockSpec(memory_space=pltpu.VMEM)
LIMIT = 56 * 2**20


def norm(values):
    values = values.astype(F32)
    center = values - jnp.mean(values, -1, keepdims=True)
    spread = jnp.mean(center * center, -1, keepdims=True)
    return (center * lax.rsqrt(spread + 1e-5)).astype(BF)


def mm(a, b):
    return jnp.dot(a, b, preferred_element_type=F32)


def value_blocks(values):
    lane = lax.broadcasted_iota(jnp.int32, (1, 128), 1) >> 5
    one = jnp.ones((values.shape[0], 128), BF)
    for h in range(HEADS):
        group = values[:, 128 * (h // 4) : 128 * (h // 4) + 128]
        yield h, jnp.concatenate([jnp.where(lane == h % 4, group, jnp.zeros_like(group)), one], -1)


def attend(q, keys, value_of):
    lane = lax.broadcasted_iota(jnp.int32, (1, 256), 1) >> 5
    halves = []
    for g in range(2):
        total = None
        for h in range(4 * g, 4 * g + 4):
            masked = jnp.where(lane == h, q, jnp.zeros_like(q))
            scores = lax.dot_general(masked, keys, NT, preferred_element_type=F32)
            highest = jnp.max(scores, -1, keepdims=True)
            weights = jnp.exp2((scores - highest) * SCALE).astype(BF)
            sums = mm(weights, value_of(h))
            part = sums[:, :128] / sums[:, 128:]
            total = part if total is None else total + part
        halves.append(total.astype(BF))
    return jnp.concatenate(halves, -1)


def row_kernel(qb, x_ref, wq_ref, wkv_ref, wo_ref, o_ref, q_s, k_s, v_s, o_s):
    rows = x_ref.shape[0]
    n = norm(x_ref[...])
    q_s[...] = mm(n, wq_ref[...]).astype(BF)
    kv = mm(n, wkv_ref[...]).astype(BF)
    k_s[...] = kv[:, :256]
    for h, block in value_blocks(kv[:, 256:]):
        v_s[h] = block

    def body(i, _):
        sl = pl.ds(pl.multiple_of(i * qb, qb), qb)
        mixed = attend(q_s[sl, :], k_s[...], lambda h: v_s[h])
        after = x_ref[sl, :].astype(F32) + mm(mixed, wo_ref[...])
        for hf in range(2):
            o_s[pl.ds(hf, qb, 2), :] = after[:, hf * 128 : hf * 128 + 128]
        o_ref[pl.ds(pl.multiple_of(i * 2 * qb, 2 * qb), 2 * qb), :] = o_s[...].astype(BF)
        return 0

    lax.fori_loop(0, rows // qb, body, 0)


def row_attention(x, wq, wkv, wo, qb=256):
    rows = x.shape[0]
    return pl.pallas_call(
        functools.partial(row_kernel, qb),
        out_shape=jax.ShapeDtypeStruct((2 * rows, 128), BF),
        in_specs=[VMEM] * 4,
        out_specs=VMEM,
        scratch_shapes=[
            pltpu.VMEM((rows, 256), BF),
            pltpu.VMEM((rows, 256), BF),
            pltpu.VMEM((HEADS, rows, 256), BF),
            pltpu.VMEM((2 * qb, 128), F32),
        ],
        compiler_params=pltpu.CompilerParams(vmem_limit_bytes=LIMIT),
        name="row_attention",
    )(x, wq, wkv, wo)


def column_kernel(lons, x_ref, wq_ref, wkv_ref, wo_ref, sel_ref, o_ref, x_s, o_s):
    x_s[...] = x_ref[...].astype(F32)
    step = 2 * lons
    lats = x_ref.shape[0] // step

    def body(b, _):
        x = jnp.concatenate([x_s[pl.ds(2 * b + hf, lats, step), :] for hf in range(2)], -1)
        n = norm(x)
        q = mm(n, wq_ref[...]).astype(BF)
        kv = mm(n, wkv_ref[...]).astype(BF)
        blocks = dict(value_blocks(kv[:, 256:]))
        mixed = attend(q, kv[:, :256], lambda h: blocks[h])
        after = (x + mm(mixed, wo_ref[...])).astype(BF)
        sent = mm(sel_ref[...], after)
        for hf in range(2):
            o_s[hf, pl.ds(b, sent.shape[0], lons), :] = sent[:, hf * 128 : hf * 128 + 128]
        return 0

    lax.fori_loop(0, lons, body, 0)
    size = o_ref.shape[1]
    for p in range(o_ref.shape[0]):
        o_ref[p] = o_s[p % 2, p // 2 * size : (p // 2 + 1) * size].astype(BF)


def column_attention(x, wq, wkv, wo, select, lons, peers):
    size = select.shape[0] // (peers // 2) * lons
    return pl.pallas_call(
        functools.partial(column_kernel, lons),
        out_shape=jax.ShapeDtypeStruct((peers, size, 128), BF),
        in_specs=[VMEM] * 5,
        out_specs=VMEM,
        scratch_shapes=[
            pltpu.VMEM(x.shape, F32),
            pltpu.VMEM((2, peers // 2 * size, 128), F32),
        ],
        compiler_params=pltpu.CompilerParams(vmem_limit_bytes=LIMIT),
        name="column_attention",
    )(x, wq, wkv, wo, select)


REACH = 15
T, S, PADT = 12, 8, 4
PHI = (
    0.7978842684056429,
    0.036334149112092734,
    -3.302669371540545e-05,
    -5.527338951263253e-05,
    3.974071180846511e-06,
    -1.3378322665984367e-07,
    1.8139279113192596e-09,
)


def gelu(v):
    square = jnp.minimum(v * v, 40.0)
    p = jnp.full_like(square, PHI[-1])
    for c in PHI[-2::-1]:
        p = p * square + c
    half = 0.5 * v
    return half + half * jnp.tanh(v * p)


def conv_kernel_body(lats, at_ref, left_ref, own_ref, right_ref, w_ref, keep_ref, send_ref, f_s, a_s, b_s, n_s):
    rows = keep_ref.shape[0]
    rows0 = 2 * rows + 2 * REACH
    first, half = at_ref[0], at_ref[1]
    size = own_ref.shape[1]
    per = size // rows0
    subs = 0
    for ref in (left_ref, own_ref, right_ref):
        for k in range(ref.shape[0]):
            f_s[subs * size : (subs + 1) * size] = ref[k].astype(F32)
            subs += 1

    def put(ref, row, t, v, reach):
        ref[row, PADT + t] = v
        if t >= T - reach:
            ref[row, PADT + t - T] = pltpu.roll(v, 1, 0)
        if t < reach:
            ref[row, PADT + t + T] = pltpu.roll(v, S - 1, 0)

    def stage(i, _):
        for t in range(T):
            start = t // per * size + i * per + t % per
            put(a_s, i, t, f_s[pl.ds(start, S, T // per * size), :], 1)
        return 0

    lax.fori_loop(0, rows0, stage, 0)

    def taps_of(level):
        out = []
        for k in range(9):
            both = w_ref[level, k : k + 1, :]
            out.append(jnp.broadcast_to(jnp.where(half == 0, both[:, :128], both[:, 128:]), (S, 128)))
        return out

    def inside(i):
        lat = first + i
        return jnp.logical_and(lat >= 0, lat < lats).astype(F32)

    src, dst = a_s, b_s
    edge = 0
    for level in range(3):
        rate = 2**level
        edge += rate
        taps = taps_of(level)

        def row(i, _, src=src, dst=dst, taps=taps, rate=rate, edge=edge, level=level):
            i = i + edge
            valid = inside(i)
            for t in range(T):
                total = None
                for a in range(3):
                    for b in range(3):
                        term = taps[3 * a + b] * src[i + (a - 1) * rate, PADT + t + (b - 1) * rate]
                        total = term if total is None else total + term
                new = (src[i, PADT + t] + gelu(total)).astype(BF).astype(F32) * valid
                if level < 2:
                    put(dst, i, t, new, 2 * rate)
                else:
                    n_s[pl.ds(i * (S * T) + t, S, T), :] = new
            return 0

        lax.fori_loop(0, rows0 - 2 * edge, row, 0)
        src, dst = dst, src

    rate = 8
    taps = taps_of(3)
    cols = keep_ref.shape[1]
    for ref, base in ((send_ref, (1 - half) * rows), (keep_ref, half * rows)):

        def last(i, _, ref=ref, base=base):
            row = base + REACH + i
            out = []
            for q in range(cols // S):
                def cell(a, b, q=q):
                    at = (row + (a - 1) * rate) * (S * T) + 2 * S + q * S + (b - 1) * rate
                    return n_s[pl.ds(pl.multiple_of(at, S), S), :]

                total = None
                for a in range(3):
                    for b in range(3):
                        term = taps[3 * a + b] * cell(a, b)
                        total = term if total is None else total + term
                out.append(cell(1, 1) + gelu(total))
            ref[i] = jnp.concatenate(out, 0).astype(BF)
            return 0

        lax.fori_loop(0, rows, last, 0)


def convolutions(at, left, own, right, taps, lats, rows, cols):
    rows0 = 2 * rows + 2 * REACH
    subs = left.shape[0] + own.shape[0] + right.shape[0]
    shape = jax.ShapeDtypeStruct((rows, cols, 128), BF)
    return pl.pallas_call(
        functools.partial(conv_kernel_body, lats),
        out_shape=(shape, shape),
        in_specs=[pl.BlockSpec(memory_space=pltpu.SMEM)] + [VMEM] * 4,
        out_specs=(VMEM, VMEM),
        scratch_shapes=[
            pltpu.VMEM((subs * own.shape[1], 128), F32),
            pltpu.VMEM((rows0, T + 2 * PADT, S, 128), F32),
            pltpu.VMEM((rows0, T + 2 * PADT, S, 128), F32),
            pltpu.VMEM((rows0 * S * T, 128), F32),
        ],
        compiler_params=pltpu.CompilerParams(vmem_limit_bytes=LIMIT),
        name="convolutions",
    )(at, left, own, right, taps)


def feed_kernel(batch, at_ref, keep_ref, got_ref, gu_ref, down_ref, o_ref):
    rows, cols, _ = keep_ref.shape
    half = at_ref[1]

    def feed(c, _):
        sl = pl.ds(c * batch, batch)
        keep = keep_ref[sl].reshape(batch * cols, 128)
        got = got_ref[sl].reshape(batch * cols, 128)
        state = jnp.concatenate(
            [jnp.where(half == 0, keep, got), jnp.where(half == 0, got, keep)], -1
        ).astype(F32)
        both = mm(norm(state), gu_ref[...])
        units = gu_ref.shape[1] // 2
        gate, up = both[:, :units], both[:, units:]
        hidden = (gate / (1.0 + jnp.exp(-gate)) * up).astype(BF)
        out = (state + mm(hidden, down_ref[...])).astype(BF)
        o_ref[sl] = out.reshape(batch, cols, 256)
        return 0

    lax.fori_loop(0, rows // batch, feed, 0)


def feed_forward(at, keep, got, gate_up, down, batch=7):
    rows, cols, _ = keep.shape
    return pl.pallas_call(
        functools.partial(feed_kernel, batch),
        out_shape=jax.ShapeDtypeStruct((rows, cols, 256), BF),
        in_specs=[pl.BlockSpec(memory_space=pltpu.SMEM)] + [VMEM] * 4,
        out_specs=VMEM,
        compiler_params=pltpu.CompilerParams(vmem_limit_bytes=LIMIT),
        name="feed_forward",
    )(at, keep, got, gate_up, down)


def selection(lats, rows):
    blocks = lats // rows
    span = 2 * rows + 2 * REACH
    pick = np.zeros((blocks // 2 * span, lats), np.float32)
    for p in range(blocks // 2):
        for r in range(span):
            lat = 2 * p * rows - REACH + r
            if 0 <= lat < lats:
                pick[p * span + r, (lat % rows) * blocks + lat // rows] = 1
    return pick.astype(BF)


def on_device(
    grid_state,
    row_query,
    row_keyval,
    row_output,
    column_query,
    column_keyval,
    column_output,
    conv_kernel,
    gate_up,
    down_proj,
):
    rows, cols, width = grid_state.shape
    n = lax.axis_size("lon")
    m = lax.axis_size("lat")
    lons = cols // m
    padded = jnp.pad(grid_state, ((0, n - rows), (0, 0), (0, 0)))
    lines = lax.all_to_all(padded, "lon", 0, 0, tiled=True).reshape(n * cols, width)
    after_rows = row_attention(lines, row_query, row_keyval, row_output)
    moved = lax.all_to_all(after_rows.reshape(n * m, 2 * lons, 128), ("lon", "lat"), 0, 0, tiled=True)
    moved = moved.reshape(-1, 128)[: rows * m * 2 * lons]
    pick = jnp.asarray(selection(rows * m, rows))
    sent = column_attention(moved, column_query, column_keyval, column_output, pick, lons, m)
    own = lax.all_to_all(sent, "lat", 0, 0, tiled=True)
    k = 16 // lons
    left = lax.ppermute(own[m - k :], "lon", [(i, (i + 1) % n) for i in range(n)])
    right = lax.ppermute(own[:k], "lon", [((i + 1) % n, i) for i in range(n)])
    mine = lax.axis_index("lat")
    at = jnp.stack([mine // 2 * (2 * rows) - REACH, mine % 2]).astype(jnp.int32)
    keep, send = convolutions(at, left, own, right, conv_kernel, rows * m, rows, cols)
    got = lax.ppermute(send, "lat", [(i, i ^ 1) for i in range(m)])
    return feed_forward(at, keep, got, gate_up, down_proj)


def solution(mesh):
    return jax.shard_map(
        on_device,
        mesh=mesh,
        in_specs=(P("lat", "lon", None), P(), P(), P(), P(), P(), P(), P(), P(), P()),
        out_specs=P("lat", "lon", None),
        check_vma=False,
    )
```

```python
import functools
import jax
import jax.numpy as jnp
import numpy as np
from jax import lax
from jax.sharding import PartitionSpec as P
from jax.experimental import pallas as pl
from jax.experimental.pallas import tpu as pltpu

BF = jnp.bfloat16
F32 = jnp.float32
HEADS = 8
NT = (((1,), (1,)), ((), ()))
SCALE = 1.4426950408889634 * 32**-0.5
VMEM = pl.BlockSpec(memory_space=pltpu.VMEM)
LIMIT = 24 * 2**20


def norm(values):
    values = values.astype(F32)
    center = values - jnp.mean(values, -1, keepdims=True)
    spread = jnp.mean(center * center, -1, keepdims=True)
    return (center * lax.rsqrt(spread + 1e-5)).astype(BF)


def mm(a, b):
    return jnp.dot(a, b, preferred_element_type=F32)


def value_blocks(values):
    lane = lax.broadcasted_iota(jnp.int32, (1, 128), 1) >> 5
    one = jnp.ones((values.shape[0], 128), BF)
    for h in range(HEADS):
        group = values[:, 128 * (h // 4) : 128 * (h // 4) + 128]
        yield h, jnp.concatenate([jnp.where(lane == h % 4, group, jnp.zeros_like(group)), one], -1)


def attend(q, keys, value_of):
    lane = lax.broadcasted_iota(jnp.int32, (1, 256), 1) >> 5
    halves = []
    for g in range(2):
        total = None
        for h in range(4 * g, 4 * g + 4):
            masked = jnp.where(lane == h, q, jnp.zeros_like(q))
            scores = lax.dot_general(masked, keys, NT, preferred_element_type=F32)
            highest = jnp.max(scores, -1, keepdims=True)
            weights = jnp.exp2((scores - highest) * SCALE).astype(BF)
            sums = mm(weights, value_of(h))
            part = sums[:, :128] / sums[:, 128:]
            total = part if total is None else total + part
        halves.append(total.astype(BF))
    return jnp.concatenate(halves, -1)


def row_kernel(qb, x_ref, wq_ref, wkv_ref, wo_ref, o_ref, q_s, k_s, v_s, o_s):
    rows = x_ref.shape[0]
    n = norm(x_ref[...])
    q_s[...] = mm(n, wq_ref[...]).astype(BF)
    kv = mm(n, wkv_ref[...]).astype(BF)
    k_s[...] = kv[:, :256]
    for h, block in value_blocks(kv[:, 256:]):
        v_s[h] = block

    def body(i, _):
        sl = pl.ds(pl.multiple_of(i * qb, qb), qb)
        mixed = attend(q_s[sl, :], k_s[...], lambda h: v_s[h])
        after = x_ref[sl, :].astype(F32) + mm(mixed, wo_ref[...])
        for hf in range(2):
            o_s[pl.ds(hf, qb, 2), :] = after[:, hf * 128 : hf * 128 + 128]
        o_ref[pl.ds(pl.multiple_of(i * 2 * qb, 2 * qb), 2 * qb), :] = o_s[...].astype(BF)
        return 0

    lax.fori_loop(0, rows // qb, body, 0)


def row_attention(x, wq, wkv, wo, qb=256):
    rows = x.shape[0]
    return pl.pallas_call(
        functools.partial(row_kernel, qb),
        out_shape=jax.ShapeDtypeStruct((2 * rows, 128), BF),
        in_specs=[VMEM] * 4,
        out_specs=VMEM,
        scratch_shapes=[
            pltpu.VMEM((rows, 256), BF),
            pltpu.VMEM((rows, 256), BF),
            pltpu.VMEM((HEADS, rows, 256), BF),
            pltpu.VMEM((2 * qb, 128), F32),
        ],
        compiler_params=pltpu.CompilerParams(vmem_limit_bytes=LIMIT),
        name="row_attention",
    )(x, wq, wkv, wo)


def column_kernel(lons, span, x_ref, wq_ref, wkv_ref, wo_ref, sel_ref, o_ref, x_s, o_s):
    step = 2 * lons
    lats = sel_ref.shape[1]
    x_s[...] = x_ref[: lats * step].astype(F32)
    size = lons * span
    blocks = o_ref.shape[0] // 2
    pitch = sel_ref.shape[0] // blocks

    def body(b, _):
        x = jnp.concatenate([x_s[pl.ds(2 * b + hf, lats, step), :] for hf in range(2)], -1)
        n = norm(x)
        q = mm(n, wq_ref[...]).astype(BF)
        kv = mm(n, wkv_ref[...]).astype(BF)
        blocks_of = dict(value_blocks(kv[:, 256:]))
        mixed = attend(q, kv[:, :256], lambda h: blocks_of[h])
        after = (x + mm(mixed, wo_ref[...])).astype(BF)
        sent = mm(sel_ref[...], after)
        for p in range(blocks):
            for hf in range(2):
                part = sent[p * pitch : p * pitch + span, hf * 128 : hf * 128 + 128]
                o_s[hf, pl.ds(p * size + b * span, span), :] = part
        return 0

    lax.fori_loop(0, lons, body, 0)
    for p in range(o_ref.shape[0]):
        o_ref[p] = o_s[p % 2, p // 2 * size : (p // 2 + 1) * size].astype(BF)


def column_attention(x, wq, wkv, wo, select, lons, span, peers):
    size = lons * span
    return pl.pallas_call(
        functools.partial(column_kernel, lons, span),
        out_shape=jax.ShapeDtypeStruct((peers, size, 128), BF),
        in_specs=[VMEM] * 5,
        out_specs=VMEM,
        scratch_shapes=[
            pltpu.VMEM((select.shape[1] * 2 * lons, 128), F32),
            pltpu.VMEM((2, peers // 2 * size, 128), F32),
        ],
        compiler_params=pltpu.CompilerParams(vmem_limit_bytes=LIMIT),
        name="column_attention",
    )(x, wq, wkv, wo, select)


REACH = 15
S = 8
HALO = 16


def gelu(v):
    half = 0.5 * v
    return half + half * lax.erf(v * 0.7071067811865476)


def taps_of(w_ref, level, half):
    out = []
    for k in range(9):
        both = w_ref[k, level : level + 1, :]
        out.append(jnp.broadcast_to(jnp.where(half == 0, both[:, :128], both[:, 128:]), (S, 128)))
    return out


def convolved(src, width, taps, i, at, rate):
    def cell(a, b):
        return src[pl.ds((i + (a - 1) * rate) * width + at + (b - 1) * rate, S), :]

    total = None
    for a in range(3):
        for b in range(3):
            term = taps[3 * a + b] * cell(a, b)
            total = term if total is None else total + term
    return (cell(1, 1) + gelu(total)).astype(BF).astype(F32)


def spread(part, buf, width, lon, rows):
    values = part.astype(F32)
    for b in range(part.shape[0] // rows):
        at = 0
        while at < rows:
            place = b * rows + at
            count = min(rows - at, S - place % S)
            buf[pl.ds(at * width + lon + b, count, width), :] = values[place : place + count]
            at += count


def position(rows):
    index = lax.axis_index("lat")
    return lax.shift_right_logical(index, 1) * (2 * rows) - REACH, lax.bitwise_and(index, 1)


def valid(first, i, lats):
    return jnp.logical_and(first + i >= 0, first + i < lats).astype(F32)


INNER = ((17, 25, 33, 41, 49, 57, 65, 71), (19, 27, 35, 43, 51, 59, 67, 69), (23, 31, 39, 47, 55, 63, 65))
OUTER = ((2, 9, 79, 86), (4, 11, 77, 84), (8, 15, 73, 80))


def inner_kernel(lats, rows, own_ref, w_ref, edge_ref, mid_ref, a_s, b_s):
    first, half = position(rows)
    rows0 = edge_ref.shape[1]
    width = own_ref.shape[0] * own_ref.shape[1] // rows0
    per = own_ref.shape[1] // rows0
    for k in range(own_ref.shape[0]):
        spread(own_ref[k], a_s, width, k * per, rows0)

    def raw(i, _):
        ends = [a_s[pl.ds(i * width + c, S), :] for c in (0, width - S)]
        edge_ref[0, i] = jnp.concatenate(ends, 0).astype(BF)
        return 0

    lax.fori_loop(0, rows0, raw, 0)
    src, dst = a_s, b_s
    edge = 0
    for level in range(3):
        rate = 2**level
        edge += rate
        taps = taps_of(w_ref, level, half)

        def row(i, _, src=src, dst=dst, taps=taps, rate=rate, edge=edge, level=level):
            i = i + edge
            mask = valid(first, i, lats)
            out = [convolved(src, width, taps, i, c - HALO, rate) * mask for c in INNER[level]]
            if level < 2:
                for c, v in zip(INNER[level], out):
                    dst[pl.ds(i * width + c - HALO, S), :] = v
                edge_ref[level + 1, i] = jnp.concatenate([out[0], out[-1]], 0).astype(BF)
            else:
                mid_ref[i - edge] = jnp.concatenate(out, 0).astype(BF)
            return 0

        lax.fori_loop(0, rows0 - 2 * edge, row, 0)
        src, dst = dst, src


def inner_levels(own, taps, lats, rows):
    rows0 = 2 * rows + 2 * REACH
    per = own.shape[0] * own.shape[1]
    return pl.pallas_call(
        functools.partial(inner_kernel, lats, rows),
        out_shape=(
            jax.ShapeDtypeStruct((3, rows0, 2 * S, 128), BF),
            jax.ShapeDtypeStruct((rows0 - 14, len(INNER[2]) * S, 128), BF),
        ),
        in_specs=[VMEM] * 2,
        out_specs=(VMEM, VMEM),
        scratch_shapes=[pltpu.VMEM((per, 128), F32)] * 2,
        compiler_params=pltpu.CompilerParams(vmem_limit_bytes=LIMIT),
        cost_estimate=pl.CostEstimate(flops=60000000, bytes_accessed=8000000, transcendentals=1000000),
        name="inner_levels",
    )(own, taps)


def outer_kernel(lats, left_ref, right_ref, edge_ref, mid_ref, w_ref, keep_ref, send_ref, *bufs):
    rows, cols, _ = keep_ref.shape
    first, half = position(rows)
    rows0 = edge_ref.shape[1]
    width = cols + 2 * HALO
    per = left_ref.shape[1] // rows0
    for k in range(left_ref.shape[0]):
        spread(left_ref[k], bufs[0], width, k * per, rows0)
        spread(right_ref[k], bufs[0], width, HALO + cols + k * per, rows0)

    def ends(i, _):
        for level in range(3):
            at = (HALO, HALO + cols - S) if level == 0 else (INNER[level - 1][0], INNER[level - 1][-1])
            both = edge_ref[level, i].astype(F32)
            for e in range(2):
                bufs[level][pl.ds(i * width + at[e], S), :] = both[e * S : e * S + S]
        return 0

    lax.fori_loop(0, rows0, ends, 0)

    def middle(i, _):
        cells = mid_ref[i].astype(F32)
        for g, c in enumerate(INNER[2]):
            bufs[3][pl.ds((i + 7) * width + c, S), :] = cells[g * S : g * S + S]
        return 0

    lax.fori_loop(0, mid_ref.shape[0], middle, 0)
    edge = 0
    for level in range(3):
        rate = 2**level
        edge += rate
        taps = taps_of(w_ref, level, half)

        def row(i, _, taps=taps, rate=rate, edge=edge, level=level):
            i = i + edge
            mask = valid(first, i, lats)
            out = [convolved(bufs[level], width, taps, i, c, rate) * mask for c in OUTER[level]]
            for c, v in zip(OUTER[level], out):
                bufs[level + 1][pl.ds(i * width + c, S), :] = v
            return 0

        lax.fori_loop(0, rows0 - 2 * edge, row, 0)

    taps = taps_of(w_ref, 3, half)
    for ref, base in ((send_ref, (1 - half) * rows), (keep_ref, half * rows)):

        def last(i, _, ref=ref, base=base):
            row = base + REACH + i
            out = [convolved(bufs[3], width, taps, row, HALO + q * S, 8) for q in range(cols // S)]
            ref[i] = jnp.concatenate(out, 0).astype(BF)
            return 0

        lax.fori_loop(0, rows, last, 0)


def outer_levels(left, right, edge, mid, taps, lats, rows, cols):
    rows0 = edge.shape[1]
    shape = jax.ShapeDtypeStruct((rows, cols, 128), BF)
    return pl.pallas_call(
        functools.partial(outer_kernel, lats),
        out_shape=(shape, shape),
        in_specs=[VMEM] * 5,
        out_specs=(VMEM, VMEM),
        scratch_shapes=[pltpu.VMEM((rows0 * (cols + 2 * HALO), 128), F32)] * 4,
        compiler_params=pltpu.CompilerParams(vmem_limit_bytes=LIMIT),
        cost_estimate=pl.CostEstimate(flops=40000000, bytes_accessed=4000000, transcendentals=500000),
        name="outer_levels",
    )(left, right, edge, mid, taps)


def feed_kernel(batch, keep_ref, got_ref, gu_ref, down_ref, o_ref):
    rows, cols, _ = keep_ref.shape
    half = lax.bitwise_and(lax.axis_index("lat"), 1)

    def feed(c, _):
        sl = pl.ds(c * batch, batch)
        keep = keep_ref[sl].reshape(batch * cols, 128)
        got = got_ref[sl].reshape(batch * cols, 128)
        state = jnp.concatenate(
            [jnp.where(half == 0, keep, got), jnp.where(half == 0, got, keep)], -1
        ).astype(F32)
        both = mm(norm(state), gu_ref[...])
        units = gu_ref.shape[1] // 2
        gate, up = both[:, :units], both[:, units:]
        hidden = (gate / (1.0 + jnp.exp(-gate)) * up).astype(BF)
        out = (state + mm(hidden, down_ref[...])).astype(BF)
        o_ref[sl] = out.reshape(batch, cols, 256)
        return 0

    lax.fori_loop(0, rows // batch, feed, 0)


def feed_forward(keep, got, gate_up, down, batch=7):
    rows, cols, _ = keep.shape
    return pl.pallas_call(
        functools.partial(feed_kernel, batch),
        out_shape=jax.ShapeDtypeStruct((rows, cols, 256), BF),
        in_specs=[VMEM] * 4,
        out_specs=VMEM,
        compiler_params=pltpu.CompilerParams(vmem_limit_bytes=LIMIT),
        name="feed_forward",
    )(keep, got, gate_up, down)


def selection(lats, rows):
    blocks = lats // rows
    span = 2 * rows + 2 * REACH
    pitch = -(-span // 16) * 16
    pick = np.zeros((blocks // 2 * pitch, lats), np.float32)
    for p in range(blocks // 2):
        for r in range(span):
            lat = 2 * p * rows - REACH + r
            if 0 <= lat < lats:
                pick[p * pitch + r, (lat % rows) * blocks + lat // rows] = 1
    return pick.astype(BF)


def on_device(
    grid_state,
    row_query,
    row_keyval,
    row_output,
    column_query,
    column_keyval,
    column_output,
    conv_kernel,
    gate_up,
    down_proj,
):
    rows, cols, width = grid_state.shape
    n = lax.axis_size("lon")
    m = lax.axis_size("lat")
    lons = cols // m
    padded = jnp.pad(grid_state, ((0, n - rows), (0, 0), (0, 0)))
    lines = lax.all_to_all(padded, "lon", 0, 0, tiled=True).reshape(n * cols, width)
    after_rows = row_attention(lines, row_query, row_keyval, row_output)
    moved = lax.all_to_all(after_rows.reshape(n * m, 2 * lons, 128), ("lon", "lat"), 0, 0, tiled=True)
    moved = moved.reshape(-1, 128)
    pick = jnp.asarray(selection(rows * m, rows))
    span = 2 * rows + 2 * REACH
    sent = column_attention(moved, column_query, column_keyval, column_output, pick, lons, span, m)
    own = lax.all_to_all(sent, "lat", 0, 0, tiled=True)
    k = HALO // lons
    left = lax.ppermute(own[m - k :], "lon", [(i, (i + 1) % n) for i in range(n)])
    right = lax.ppermute(own[:k], "lon", [((i + 1) % n, i) for i in range(n)])
    taps = jnp.swapaxes(conv_kernel, 0, 1)
    edge, mid = inner_levels(own, taps, rows * m, rows)
    keep, send = outer_levels(left, right, edge, mid, taps, rows * m, rows, cols)
    got = lax.ppermute(send, "lat", [(i, i ^ 1) for i in range(m)])
    return feed_forward(keep, got, gate_up, down_proj)


def solution(mesh):
    return jax.shard_map(
        on_device,
        mesh=mesh,
        in_specs=(P("lat", "lon", None), P(), P(), P(), P(), P(), P(), P(), P(), P()),
        out_specs=P("lat", "lon", None),
        check_vma=False,
    )
```

```python
import functools
import jax
import jax.numpy as jnp
import numpy as np
from jax import lax
from jax.sharding import PartitionSpec as P
from jax.experimental import pallas as pl
from jax.experimental.pallas import tpu as pltpu

BF = jnp.bfloat16
F32 = jnp.float32
HEADS = 8
NT = (((1,), (1,)), ((), ()))
SCALE = 1.4426950408889634 * 32**-0.5
VMEM = pl.BlockSpec(memory_space=pltpu.VMEM)
LIMIT = 24 * 2**20


def norm(values):
    values = values.astype(F32)
    center = values - jnp.mean(values, -1, keepdims=True)
    spread = jnp.mean(center * center, -1, keepdims=True)
    return (center * lax.rsqrt(spread + 1e-5)).astype(BF)


def mm(a, b):
    return jnp.dot(a, b, preferred_element_type=F32)


def value_blocks(values):
    lane = lax.broadcasted_iota(jnp.int32, (1, 128), 1) >> 5
    one = jnp.ones((values.shape[0], 128), BF)
    for h in range(HEADS):
        group = values[:, 128 * (h // 4) : 128 * (h // 4) + 128]
        yield h, jnp.concatenate([jnp.where(lane == h % 4, group, jnp.zeros_like(group)), one], -1)


def attend(q, keys, value_of):
    lane = lax.broadcasted_iota(jnp.int32, (1, 256), 1) >> 5

    def scores_of(h):
        masked = jnp.where(lane == h, q, jnp.zeros_like(q))
        return lax.dot_general(masked, keys, NT, preferred_element_type=F32)

    halves = []
    later = scores_of(0)
    for g in range(2):
        total = None
        for h in range(4 * g, 4 * g + 4):
            scores = later
            if h + 1 < HEADS:
                later = scores_of(h + 1)
            highest = jnp.max(scores, -1, keepdims=True)
            weights = jnp.exp2((scores - highest) * SCALE).astype(BF)
            sums = mm(weights, value_of(h))
            part = sums[:, :128] / sums[:, 128:]
            total = part if total is None else total + part
        halves.append(total.astype(BF))
    return jnp.concatenate(halves, -1)


def row_kernel(qb, x_ref, wq_ref, wkv_ref, wo_ref, o_ref, q_s, k_s, v_s, o_s):
    rows = x_ref.shape[0]
    n = norm(x_ref[...])
    q_s[...] = mm(n, wq_ref[...]).astype(BF)
    kv = mm(n, wkv_ref[...]).astype(BF)
    k_s[...] = kv[:, :256]
    for h, block in value_blocks(kv[:, 256:]):
        v_s[h] = block

    def body(i, _):
        sl = pl.ds(pl.multiple_of(i * qb, qb), qb)
        mixed = attend(q_s[sl, :], k_s[...], lambda h: v_s[h])
        after = x_ref[sl, :].astype(F32) + mm(mixed, wo_ref[...])
        for hf in range(2):
            o_s[pl.ds(hf, qb, 2), :] = after[:, hf * 128 : hf * 128 + 128]
        o_ref[pl.ds(pl.multiple_of(i * 2 * qb, 2 * qb), 2 * qb), :] = o_s[...].astype(BF)
        return 0

    lax.fori_loop(0, rows // qb, body, 0)


def row_attention(x, wq, wkv, wo, qb=512):
    rows = x.shape[0]
    return pl.pallas_call(
        functools.partial(row_kernel, qb),
        out_shape=jax.ShapeDtypeStruct((2 * rows, 128), BF),
        in_specs=[VMEM] * 4,
        out_specs=VMEM,
        scratch_shapes=[
            pltpu.VMEM((rows, 256), BF),
            pltpu.VMEM((rows, 256), BF),
            pltpu.VMEM((HEADS, rows, 256), BF),
            pltpu.VMEM((2 * qb, 128), F32),
        ],
        compiler_params=pltpu.CompilerParams(vmem_limit_bytes=LIMIT),
        name="row_attention",
    )(x, wq, wkv, wo)


def column_kernel(lons, span, unroll, x_ref, wq_ref, wkv_ref, wo_ref, sel_ref, o_ref, x_s, o_s):
    step = 2 * lons
    lats = sel_ref.shape[1]
    x_s[...] = x_ref[: lats * step].astype(F32)
    size = lons * span
    blocks = o_ref.shape[0] // 2
    pitch = sel_ref.shape[0] // blocks

    def body(b, _):
        x = jnp.concatenate([x_s[pl.ds(2 * b + hf, lats, step), :] for hf in range(2)], -1)
        n = norm(x)
        q = mm(n, wq_ref[...]).astype(BF)
        kv = mm(n, wkv_ref[...]).astype(BF)
        blocks_of = dict(value_blocks(kv[:, 256:]))
        mixed = attend(q, kv[:, :256], lambda h: blocks_of[h])
        after = (x + mm(mixed, wo_ref[...])).astype(BF)
        sent = mm(sel_ref[...], after)
        for p in range(blocks):
            for hf in range(2):
                part = sent[p * pitch : p * pitch + span, hf * 128 : hf * 128 + 128]
                o_s[hf, pl.ds(p * size + b * span, span), :] = part
        return 0

    if unroll == lons:
        for b in range(lons):
            body(b, 0)
    else:
        lax.fori_loop(0, lons, body, 0, unroll=unroll)
    for p in range(o_ref.shape[0]):
        o_ref[p] = o_s[p % 2, p // 2 * size : (p // 2 + 1) * size].astype(BF)


def column_attention(x, wq, wkv, wo, select, lons, span, peers, unroll=4):
    size = lons * span
    return pl.pallas_call(
        functools.partial(column_kernel, lons, span, unroll),
        out_shape=jax.ShapeDtypeStruct((peers, size, 128), BF),
        in_specs=[VMEM] * 5,
        out_specs=VMEM,
        scratch_shapes=[
            pltpu.VMEM((select.shape[1] * 2 * lons, 128), F32),
            pltpu.VMEM((2, peers // 2 * size, 128), F32),
        ],
        compiler_params=pltpu.CompilerParams(vmem_limit_bytes=LIMIT),
        name="column_attention",
    )(x, wq, wkv, wo, select)


REACH = 15
U_IN, U_OUT, U_LAST = 4, 4, 7
S = 8
HALO = 16


ROOT_HALF = 0.7071067811865476


def taps_of(w_ref, level, half):
    out = []
    for k in range(9):
        both = w_ref[k, level : level + 1, :]
        mine = jnp.where(half == 0, both[:, :128], both[:, 128:])
        out.append(jnp.broadcast_to(mine * ROOT_HALF, (S, 128)))
    return out


def convolved(src, width, taps, i, at, rate):
    def cell(a, b):
        return src[pl.ds((i + (a - 1) * rate) * width + at + (b - 1) * rate, S), :]

    lines = []
    for a in range(3):
        terms = [taps[3 * a + b] * cell(a, b) for b in range(3)]
        lines.append(terms[0] + terms[1] + terms[2])
    total = lines[0] + lines[1] + lines[2]
    part = ROOT_HALF * total
    return (cell(1, 1) + part + part * lax.erf(total)).astype(BF)


def spread(part, buf, width, lon, rows):
    values = part.astype(F32)
    for b in range(part.shape[0] // rows):
        at = 0
        while at < rows:
            place = b * rows + at
            count = min(rows - at, S - place % S)
            buf[pl.ds(at * width + lon + b, count, width), :] = values[place : place + count]
            at += count


def position(rows):
    index = lax.axis_index("lat")
    return lax.shift_right_logical(index, 1) * (2 * rows) - REACH, lax.bitwise_and(index, 1)


def clear_outside(first, rows0, lats, clear):
    def one(i, _):
        clear(i)
        return 0

    @pl.when(first < 0)
    def _():
        lax.fori_loop(0, REACH, one, 0)

    @pl.when(first + rows0 > lats)
    def _():
        lax.fori_loop(rows0 - REACH, rows0, one, 0)


INNER = ((17, 25, 33, 41, 49, 57, 65, 71), (19, 27, 35, 43, 51, 59, 67, 69), (23, 31, 39, 47, 55, 63, 65))
OUTER = ((2, 9, 79, 86), (4, 11, 77, 84), (8, 15, 73, 80))


def inner_kernel(lats, rows, own_ref, w_ref, edge_ref, mid_ref, a_s, b_s):
    first, half = position(rows)
    rows0 = edge_ref.shape[1]
    width = own_ref.shape[0] * own_ref.shape[1] // rows0
    per = own_ref.shape[1] // rows0
    for k in range(own_ref.shape[0]):
        spread(own_ref[k], a_s, width, k * per, rows0)

    def raw(i, _):
        ends = [a_s[pl.ds(i * width + c, S), :] for c in (0, width - S)]
        edge_ref[0, i] = jnp.concatenate(ends, 0).astype(BF)
        return 0

    lax.fori_loop(0, rows0, raw, 0, unroll=2)
    src, dst = a_s, b_s
    edge = 0
    for level in range(3):
        rate = 2**level
        edge += rate
        taps = taps_of(w_ref, level, half)

        def row(i, _, src=src, dst=dst, taps=taps, rate=rate, edge=edge, level=level):
            i = i + edge
            out = [convolved(src, width, taps, i, c - HALO, rate) for c in INNER[level]]
            if level < 2:
                for c, v in zip(INNER[level], out):
                    dst[pl.ds(i * width + c - HALO, S), :] = v.astype(F32)
                edge_ref[level + 1, i] = jnp.concatenate([out[0], out[-1]], 0)
            else:
                mid_ref[i - edge] = jnp.concatenate(out, 0)
            return 0

        lax.fori_loop(0, rows0 - 2 * edge, row, 0, unroll=U_IN)

        def clear(i, dst=dst, level=level):
            if level < 2:
                for c in range(0, width, S):
                    dst[pl.ds(i * width + c, S), :] = jnp.zeros((S, 128), F32)

        clear_outside(first, rows0, lats, clear)
        src, dst = dst, src


def inner_levels(own, taps, lats, rows):
    rows0 = 2 * rows + 2 * REACH
    per = own.shape[0] * own.shape[1]
    return pl.pallas_call(
        functools.partial(inner_kernel, lats, rows),
        out_shape=(
            jax.ShapeDtypeStruct((3, rows0, 2 * S, 128), BF),
            jax.ShapeDtypeStruct((rows0 - 14, len(INNER[2]) * S, 128), BF),
        ),
        in_specs=[VMEM] * 2,
        out_specs=(VMEM, VMEM),
        scratch_shapes=[pltpu.VMEM((per, 128), F32)] * 2,
        compiler_params=pltpu.CompilerParams(vmem_limit_bytes=LIMIT),
        cost_estimate=pl.CostEstimate(flops=60000000, bytes_accessed=8000000, transcendentals=1000000),
        name="inner_levels",
    )(own, taps)


def outer_kernel(lats, left_ref, right_ref, edge_ref, mid_ref, w_ref, keep_ref, send_ref, *bufs):
    rows, cols, _ = keep_ref.shape
    first, half = position(rows)
    rows0 = edge_ref.shape[1]
    width = cols + 2 * HALO
    per = left_ref.shape[1] // rows0
    for k in range(left_ref.shape[0]):
        spread(left_ref[k], bufs[0], width, k * per, rows0)
        spread(right_ref[k], bufs[0], width, HALO + cols + k * per, rows0)

    def ends(i, _):
        for level in range(3):
            at = (HALO, HALO + cols - S) if level == 0 else (INNER[level - 1][0], INNER[level - 1][-1])
            both = edge_ref[level, i].astype(F32)
            for e in range(2):
                bufs[level][pl.ds(i * width + at[e], S), :] = both[e * S : e * S + S]
        return 0

    lax.fori_loop(0, rows0, ends, 0, unroll=2)

    def middle(i, _):
        cells = mid_ref[i].astype(F32)
        for g, c in enumerate(INNER[2]):
            bufs[3][pl.ds((i + 7) * width + c, S), :] = cells[g * S : g * S + S]
        return 0

    lax.fori_loop(0, mid_ref.shape[0], middle, 0, unroll=4)
    edge = 0
    for level in range(3):
        rate = 2**level
        edge += rate
        taps = taps_of(w_ref, level, half)

        def row(i, _, taps=taps, rate=rate, edge=edge, level=level):
            i = i + edge
            out = [convolved(bufs[level], width, taps, i, c, rate) for c in OUTER[level]]
            for c, v in zip(OUTER[level], out):
                bufs[level + 1][pl.ds(i * width + c, S), :] = v.astype(F32)
            return 0

        lax.fori_loop(0, rows0 - 2 * edge, row, 0, unroll=U_OUT)

        def clear(i, level=level):
            for c in range(0, width, S):
                bufs[level + 1][pl.ds(i * width + c, S), :] = jnp.zeros((S, 128), F32)

        clear_outside(first, rows0, lats, clear)

    taps = taps_of(w_ref, 3, half)
    for ref, base in ((send_ref, (1 - half) * rows), (keep_ref, half * rows)):

        def last(i, _, ref=ref, base=base):
            row = base + REACH + i
            out = [convolved(bufs[3], width, taps, row, HALO + q * S, 8) for q in range(cols // S)]
            ref[i] = jnp.concatenate(out, 0)
            return 0

        lax.fori_loop(0, rows, last, 0, unroll=U_LAST)


def outer_levels(left, right, edge, mid, taps, lats, rows, cols):
    rows0 = edge.shape[1]
    shape = jax.ShapeDtypeStruct((rows, cols, 128), BF)
    return pl.pallas_call(
        functools.partial(outer_kernel, lats),
        out_shape=(shape, shape),
        in_specs=[VMEM] * 5,
        out_specs=(VMEM, VMEM),
        scratch_shapes=[pltpu.VMEM((rows0 * (cols + 2 * HALO), 128), F32)] * 4,
        compiler_params=pltpu.CompilerParams(vmem_limit_bytes=LIMIT),
        cost_estimate=pl.CostEstimate(flops=40000000, bytes_accessed=4000000, transcendentals=500000),
        name="outer_levels",
    )(left, right, edge, mid, taps)


def feed_kernel(batch, keep_ref, got_ref, gu_ref, down_ref, o_ref):
    rows, cols, _ = keep_ref.shape
    half = lax.bitwise_and(lax.axis_index("lat"), 1)

    def feed(c, _):
        sl = pl.ds(c * batch, batch)
        keep = keep_ref[sl].reshape(batch * cols, 128)
        got = got_ref[sl].reshape(batch * cols, 128)
        state = jnp.concatenate(
            [jnp.where(half == 0, keep, got), jnp.where(half == 0, got, keep)], -1
        ).astype(F32)
        both = mm(norm(state), gu_ref[...])
        units = gu_ref.shape[1] // 2
        gate, up = both[:, :units], both[:, units:]
        hidden = (gate / (1.0 + jnp.exp(-gate)) * up).astype(BF)
        out = (state + mm(hidden, down_ref[...])).astype(BF)
        o_ref[sl] = out.reshape(batch, cols, 256)
        return 0

    lax.fori_loop(0, rows // batch, feed, 0)


def feed_forward(keep, got, gate_up, down, batch=14):
    rows, cols, _ = keep.shape
    return pl.pallas_call(
        functools.partial(feed_kernel, batch),
        out_shape=jax.ShapeDtypeStruct((rows, cols, 256), BF),
        in_specs=[VMEM] * 4,
        out_specs=VMEM,
        compiler_params=pltpu.CompilerParams(vmem_limit_bytes=LIMIT),
        name="feed_forward",
    )(keep, got, gate_up, down)


def selection(lats, rows):
    blocks = lats // rows
    span = 2 * rows + 2 * REACH
    pitch = -(-span // 16) * 16
    pick = np.zeros((blocks // 2 * pitch, lats), np.float32)
    for p in range(blocks // 2):
        for r in range(span):
            lat = 2 * p * rows - REACH + r
            if 0 <= lat < lats:
                pick[p * pitch + r, (lat % rows) * blocks + lat // rows] = 1
    return pick.astype(BF)


def on_device(
    grid_state,
    row_query,
    row_keyval,
    row_output,
    column_query,
    column_keyval,
    column_output,
    conv_kernel,
    gate_up,
    down_proj,
):
    rows, cols, width = grid_state.shape
    n = lax.axis_size("lon")
    m = lax.axis_size("lat")
    lons = cols // m
    padded = jnp.pad(grid_state, ((0, n - rows), (0, 0), (0, 0)))
    lines = lax.all_to_all(padded, "lon", 0, 0, tiled=True).reshape(n * cols, width)
    after_rows = row_attention(lines, row_query, row_keyval, row_output)
    moved = lax.all_to_all(after_rows.reshape(n * m, 2 * lons, 128), ("lon", "lat"), 0, 0, tiled=True)
    moved = moved.reshape(-1, 128)
    pick = jnp.asarray(selection(rows * m, rows))
    span = 2 * rows + 2 * REACH
    sent = column_attention(moved, column_query, column_keyval, column_output, pick, lons, span, m)
    own = lax.all_to_all(sent, "lat", 0, 0, tiled=True)
    k = HALO // lons
    left = lax.ppermute(own[m - k :], "lon", [(i, (i + 1) % n) for i in range(n)])
    right = lax.ppermute(own[:k], "lon", [((i + 1) % n, i) for i in range(n)])
    taps = jnp.swapaxes(conv_kernel, 0, 1)
    edge, mid = inner_levels(own, taps, rows * m, rows)
    keep, send = outer_levels(left, right, edge, mid, taps, rows * m, rows, cols)
    got = lax.ppermute(send, "lat", [(i, i ^ 1) for i in range(m)])
    return feed_forward(keep, got, gate_up, down_proj)


def solution(mesh):
    return jax.shard_map(
        on_device,
        mesh=mesh,
        in_specs=(P("lat", "lon", None), P(), P(), P(), P(), P(), P(), P(), P(), P()),
        out_specs=P("lat", "lon", None),
        check_vma=False,
    )
```

```python
import functools
import jax
import jax.numpy as jnp
import numpy as np
from jax import lax
from jax.sharding import PartitionSpec as P
from jax.experimental import pallas as pl
from jax.experimental.pallas import tpu as pltpu

BF = jnp.bfloat16
F32 = jnp.float32
HEADS = 8
NT = (((1,), (1,)), ((), ()))
SCALE = 1.4426950408889634 * 32**-0.5
VMEM = pl.BlockSpec(memory_space=pltpu.VMEM)
LIMIT = 24 * 2**20


def norm(values):
    values = values.astype(F32)
    center = values - jnp.mean(values, -1, keepdims=True)
    spread = jnp.mean(center * center, -1, keepdims=True)
    return (center * lax.rsqrt(spread + 1e-5)).astype(BF)


def mm(a, b):
    return jnp.dot(a, b, preferred_element_type=F32)


def value_rows(values):
    turned = jnp.transpose(values)
    one = jnp.ones((16, values.shape[0]), BF)
    return [jnp.concatenate([turned[32 * h : 32 * h + 32], one], 0) for h in range(HEADS)]


def attend(q, keys, value_of, pieces=2):
    lane = lax.broadcasted_iota(jnp.int32, (1, 256), 1) >> 5
    size = q.shape[0] // pieces

    def scores_of(h, z):
        some = q[z * size : z * size + size]
        masked = jnp.where(lane == h, some, jnp.zeros_like(some))
        return lax.dot_general(keys, masked, NT, preferred_element_type=F32)

    order = [(h, z) for h in range(HEADS) for z in range(pieces)]
    parts = [[] for _ in range(pieces)]
    later = scores_of(*order[0])
    for at, (h, z) in enumerate(order):
        scores = later
        if at + 1 < len(order):
            later = scores_of(*order[at + 1])
        highest = jnp.max(scores, 0, keepdims=True)
        weights = jnp.exp2((scores - highest) * SCALE).astype(BF)
        sums = mm(value_of(h), weights)
        parts[z].append(sums[:32] / sums[32:33])
    whole = jnp.concatenate([jnp.concatenate(p, 0) for p in parts], 1)
    return jnp.transpose(whole).astype(BF)


def value_blocks(values):
    lane = lax.broadcasted_iota(jnp.int32, (1, 128), 1) >> 5
    one = jnp.ones((values.shape[0], 128), BF)
    blocks = []
    for h in range(HEADS):
        group = values[:, 128 * (h // 4) : 128 * (h // 4) + 128]
        blocks.append(jnp.concatenate([jnp.where(lane == h % 4, group, jnp.zeros_like(group)), one], -1))
    return blocks


def attend_short(q, keys, values):
    lane = lax.broadcasted_iota(jnp.int32, (1, 256), 1) >> 5
    blocks = value_blocks(values)

    def scores_of(h):
        masked = jnp.where(lane == h, q, jnp.zeros_like(q))
        return lax.dot_general(masked, keys, NT, preferred_element_type=F32)

    halves = []
    later = scores_of(0)
    for g in range(2):
        total = None
        for h in range(4 * g, 4 * g + 4):
            scores = later
            if h + 1 < HEADS:
                later = scores_of(h + 1)
            highest = jnp.max(scores, -1, keepdims=True)
            weights = jnp.exp2((scores - highest) * SCALE).astype(BF)
            sums = mm(weights, blocks[h])
            part = sums[:, :128] / sums[:, 128:]
            total = part if total is None else total + part
        halves.append(total.astype(BF))
    return jnp.concatenate(halves, -1)


def row_kernel(qb, x_ref, wq_ref, wkv_ref, wo_ref, o_ref, q_s, k_s, v_s, o_s):
    rows = x_ref.shape[0]
    n = norm(x_ref[...])
    q_s[...] = mm(n, wq_ref[...]).astype(BF)
    kv = mm(n, wkv_ref[...]).astype(BF)
    k_s[...] = kv[:, :256]
    for h, block in enumerate(value_rows(kv[:, 256:])):
        v_s[h] = block

    def body(i, _):
        sl = pl.ds(pl.multiple_of(i * qb, qb), qb)
        mixed = attend(q_s[sl, :], k_s[...], lambda h: v_s[h])
        after = x_ref[sl, :].astype(F32) + mm(mixed, wo_ref[...])
        for hf in range(2):
            o_s[pl.ds(hf, qb, 2), :] = after[:, hf * 128 : hf * 128 + 128]
        o_ref[pl.ds(pl.multiple_of(i * 2 * qb, 2 * qb), 2 * qb), :] = o_s[...].astype(BF)
        return 0

    lax.fori_loop(0, rows // qb, body, 0)


def row_attention(x, wq, wkv, wo, qb=1024):
    rows = x.shape[0]
    return pl.pallas_call(
        functools.partial(row_kernel, qb),
        out_shape=jax.ShapeDtypeStruct((2 * rows, 128), BF),
        in_specs=[VMEM] * 4,
        out_specs=VMEM,
        scratch_shapes=[
            pltpu.VMEM((rows, 256), BF),
            pltpu.VMEM((rows, 256), BF),
            pltpu.VMEM((HEADS, 48, rows), BF),
            pltpu.VMEM((2 * qb, 128), F32),
        ],
        compiler_params=pltpu.CompilerParams(vmem_limit_bytes=LIMIT),
        name="row_attention",
    )(x, wq, wkv, wo)


def column_kernel(lons, span, unroll, x_ref, wq_ref, wkv_ref, wo_ref, sel_ref, o_ref, x_s, o_s):
    step = 2 * lons
    lats = sel_ref.shape[1]
    x_s[...] = x_ref[: lats * step].astype(F32)
    size = lons * span
    blocks = o_ref.shape[0] // 2
    pitch = sel_ref.shape[0] // blocks

    def body(b, _):
        x = jnp.concatenate([x_s[pl.ds(2 * b + hf, lats, step), :] for hf in range(2)], -1)
        n = norm(x)
        q = mm(n, wq_ref[...]).astype(BF)
        kv = mm(n, wkv_ref[...]).astype(BF)
        mixed = attend_short(q, kv[:, :256], kv[:, 256:])
        after = (x + mm(mixed, wo_ref[...])).astype(BF)
        sent = mm(sel_ref[...], after)
        for p in range(blocks):
            for hf in range(2):
                part = sent[p * pitch : p * pitch + span, hf * 128 : hf * 128 + 128]
                o_s[hf, pl.ds(p * size + b * span, span), :] = part
        return 0

    if unroll == lons:
        for b in range(lons):
            body(b, 0)
    else:
        lax.fori_loop(0, lons, body, 0, unroll=unroll)
    for p in range(o_ref.shape[0]):
        o_ref[p] = o_s[p % 2, p // 2 * size : (p // 2 + 1) * size].astype(BF)


def column_attention(x, wq, wkv, wo, select, lons, span, peers, unroll=4):
    size = lons * span
    return pl.pallas_call(
        functools.partial(column_kernel, lons, span, unroll),
        out_shape=jax.ShapeDtypeStruct((peers, size, 128), BF),
        in_specs=[VMEM] * 5,
        out_specs=VMEM,
        scratch_shapes=[
            pltpu.VMEM((select.shape[1] * 2 * lons, 128), F32),
            pltpu.VMEM((2, peers // 2 * size, 128), F32),
        ],
        compiler_params=pltpu.CompilerParams(vmem_limit_bytes=LIMIT),
        name="column_attention",
    )(x, wq, wkv, wo, select)


REACH = 15
U_IN, U_OUT, U_LAST = 4, 4, 7
S = 8
HALO = 16


ROOT_HALF = 0.7071067811865476


def taps_of(w_ref, level, half):
    out = []
    for k in range(9):
        both = w_ref[k, level : level + 1, :]
        mine = jnp.where(half == 0, both[:, :128], both[:, 128:])
        out.append(jnp.broadcast_to(mine * ROOT_HALF, (S, 128)))
    return out


def convolved(src, width, taps, i, at, rate):
    def cell(a, b):
        return src[pl.ds((i + (a - 1) * rate) * width + at + (b - 1) * rate, S), :]

    lines = []
    for a in range(3):
        terms = [taps[3 * a + b] * cell(a, b) for b in range(3)]
        lines.append(terms[0] + terms[1] + terms[2])
    total = lines[0] + lines[1] + lines[2]
    part = ROOT_HALF * total
    return (cell(1, 1) + part + part * lax.erf(total)).astype(BF)


def spread(part, buf, width, lon, rows):
    values = part.astype(F32)
    for b in range(part.shape[0] // rows):
        at = 0
        while at < rows:
            place = b * rows + at
            count = min(rows - at, S - place % S)
            buf[pl.ds(at * width + lon + b, count, width), :] = values[place : place + count]
            at += count


def position(rows):
    index = lax.axis_index("lat")
    return lax.shift_right_logical(index, 1) * (2 * rows) - REACH, lax.bitwise_and(index, 1)


def clear_outside(first, rows0, lats, clear):
    def one(i, _):
        clear(i)
        return 0

    @pl.when(first < 0)
    def _():
        lax.fori_loop(0, REACH, one, 0)

    @pl.when(first + rows0 > lats)
    def _():
        lax.fori_loop(rows0 - REACH, rows0, one, 0)


INNER = ((17, 25, 33, 41, 49, 57, 65, 71), (19, 27, 35, 43, 51, 59, 67, 69), (23, 31, 39, 47, 55, 63, 65))
MIDDLE = (2, 3, 4, 5)
OUTER = ((2, 9, 79, 86), (4, 11, 77, 84), (8, 15, 73, 80))


def inner_kernel(lats, rows, own_ref, w_ref, edge_ref, mid_ref, done_ref, a_s, b_s):
    first, half = position(rows)
    rows0 = edge_ref.shape[1]
    width = own_ref.shape[0] * own_ref.shape[1] // rows0
    per = own_ref.shape[1] // rows0
    for k in range(own_ref.shape[0]):
        spread(own_ref[k], a_s, width, k * per, rows0)

    def raw(i, _):
        ends = [a_s[pl.ds(i * width + c, S), :] for c in (0, width - S)]
        edge_ref[0, i] = jnp.concatenate(ends, 0).astype(BF)
        return 0

    lax.fori_loop(0, rows0, raw, 0, unroll=2)
    src, dst = a_s, b_s
    edge = 0
    for level in range(3):
        rate = 2**level
        edge += rate
        taps = taps_of(w_ref, level, half)

        def row(i, _, src=src, dst=dst, taps=taps, rate=rate, edge=edge, level=level):
            i = i + edge
            out = [convolved(src, width, taps, i, c - HALO, rate) for c in INNER[level]]
            for c, v in zip(INNER[level], out):
                dst[pl.ds(i * width + c - HALO, S), :] = v.astype(F32)
            if level < 2:
                edge_ref[level + 1, i] = jnp.concatenate([out[0], out[-1]], 0)
            else:
                mid_ref[i - edge] = jnp.concatenate(out, 0)
            return 0

        lax.fori_loop(0, rows0 - 2 * edge, row, 0, unroll=U_IN)

        def clear(i, dst=dst):
            for c in range(0, width, S):
                dst[pl.ds(i * width + c, S), :] = jnp.zeros((S, 128), F32)

        clear_outside(first, rows0, lats, clear)
        src, dst = dst, src

    taps = taps_of(w_ref, 3, half)

    def last(i, _):
        out = [convolved(src, width, taps, i + REACH, q * S, 8) for q in MIDDLE]
        done_ref[i] = jnp.concatenate(out, 0)
        return 0

    lax.fori_loop(0, 2 * rows, last, 0, unroll=U_LAST)


def inner_levels(own, taps, lats, rows):
    rows0 = 2 * rows + 2 * REACH
    per = own.shape[0] * own.shape[1]
    return pl.pallas_call(
        functools.partial(inner_kernel, lats, rows),
        out_shape=(
            jax.ShapeDtypeStruct((3, rows0, 2 * S, 128), BF),
            jax.ShapeDtypeStruct((rows0 - 14, len(INNER[2]) * S, 128), BF),
            jax.ShapeDtypeStruct((2 * rows, len(MIDDLE) * S, 128), BF),
        ),
        in_specs=[VMEM] * 2,
        out_specs=(VMEM, VMEM, VMEM),
        scratch_shapes=[pltpu.VMEM((per, 128), F32)] * 2,
        compiler_params=pltpu.CompilerParams(vmem_limit_bytes=LIMIT),
        cost_estimate=pl.CostEstimate(flops=60000000, bytes_accessed=8000000, transcendentals=1000000),
        name="inner_levels",
    )(own, taps)


def outer_kernel(lats, left_ref, right_ref, edge_ref, mid_ref, done_ref, w_ref, keep_ref, send_ref, *bufs):
    rows, cols, _ = keep_ref.shape
    first, half = position(rows)
    rows0 = edge_ref.shape[1]
    width = cols + 2 * HALO
    per = left_ref.shape[1] // rows0
    for k in range(left_ref.shape[0]):
        spread(left_ref[k], bufs[0], width, k * per, rows0)
        spread(right_ref[k], bufs[0], width, HALO + cols + k * per, rows0)

    def ends(i, _):
        for level in range(3):
            at = (HALO, HALO + cols - S) if level == 0 else (INNER[level - 1][0], INNER[level - 1][-1])
            both = edge_ref[level, i].astype(F32)
            for e in range(2):
                bufs[level][pl.ds(i * width + at[e], S), :] = both[e * S : e * S + S]
        return 0

    lax.fori_loop(0, rows0, ends, 0, unroll=2)

    def middle(i, _):
        cells = mid_ref[i].astype(F32)
        for g, c in enumerate(INNER[2]):
            bufs[3][pl.ds((i + 7) * width + c, S), :] = cells[g * S : g * S + S]
        return 0

    lax.fori_loop(0, mid_ref.shape[0], middle, 0, unroll=4)
    edge = 0
    for level in range(3):
        rate = 2**level
        edge += rate
        taps = taps_of(w_ref, level, half)

        def row(i, _, taps=taps, rate=rate, edge=edge, level=level):
            i = i + edge
            out = [convolved(bufs[level], width, taps, i, c, rate) for c in OUTER[level]]
            for c, v in zip(OUTER[level], out):
                bufs[level + 1][pl.ds(i * width + c, S), :] = v.astype(F32)
            return 0

        lax.fori_loop(0, rows0 - 2 * edge, row, 0, unroll=U_OUT)

        def clear(i, level=level):
            for c in range(0, width, S):
                bufs[level + 1][pl.ds(i * width + c, S), :] = jnp.zeros((S, 128), F32)

        clear_outside(first, rows0, lats, clear)

    taps = taps_of(w_ref, 3, half)
    for ref, base in ((send_ref, (1 - half) * rows), (keep_ref, half * rows)):

        def last(i, _, ref=ref, base=base):
            row = base + REACH + i
            out = [
                done_ref[base + i] if q == MIDDLE[0] else convolved(bufs[3], width, taps, row, HALO + q * S, 8)
                for q in range(cols // S)
                if q not in MIDDLE[1:]
            ]
            ref[i] = jnp.concatenate(out, 0)
            return 0

        lax.fori_loop(0, rows, last, 0, unroll=U_LAST)


def outer_levels(left, right, edge, mid, done, taps, lats, rows, cols):
    rows0 = edge.shape[1]
    shape = jax.ShapeDtypeStruct((rows, cols, 128), BF)
    return pl.pallas_call(
        functools.partial(outer_kernel, lats),
        out_shape=(shape, shape),
        in_specs=[VMEM] * 6,
        out_specs=(VMEM, VMEM),
        scratch_shapes=[pltpu.VMEM((rows0 * (cols + 2 * HALO), 128), F32)] * 4,
        compiler_params=pltpu.CompilerParams(vmem_limit_bytes=LIMIT),
        cost_estimate=pl.CostEstimate(flops=40000000, bytes_accessed=4000000, transcendentals=500000),
        name="outer_levels",
    )(left, right, edge, mid, done, taps)


def feed_kernel(batch, keep_ref, got_ref, gu_ref, down_ref, o_ref):
    rows, cols, _ = keep_ref.shape
    half = lax.bitwise_and(lax.axis_index("lat"), 1)

    def feed(c, _):
        sl = pl.ds(c * batch, batch)
        keep = keep_ref[sl].reshape(batch * cols, 128)
        got = got_ref[sl].reshape(batch * cols, 128)
        state = jnp.concatenate(
            [jnp.where(half == 0, keep, got), jnp.where(half == 0, got, keep)], -1
        ).astype(F32)
        both = mm(norm(state), gu_ref[...])
        units = gu_ref.shape[1] // 2
        gate, up = both[:, :units], both[:, units:]
        hidden = (gate / (1.0 + jnp.exp(-gate)) * up).astype(BF)
        out = (state + mm(hidden, down_ref[...])).astype(BF)
        o_ref[sl] = out.reshape(batch, cols, 256)
        return 0

    lax.fori_loop(0, rows // batch, feed, 0)


def feed_forward(keep, got, gate_up, down, batch=14):
    rows, cols, _ = keep.shape
    return pl.pallas_call(
        functools.partial(feed_kernel, batch),
        out_shape=jax.ShapeDtypeStruct((rows, cols, 256), BF),
        in_specs=[VMEM] * 4,
        out_specs=VMEM,
        compiler_params=pltpu.CompilerParams(vmem_limit_bytes=LIMIT),
        name="feed_forward",
    )(keep, got, gate_up, down)


def selection(lats, rows):
    blocks = lats // rows
    span = 2 * rows + 2 * REACH
    pitch = -(-span // 16) * 16
    pick = np.zeros((blocks // 2 * pitch, lats), np.float32)
    for p in range(blocks // 2):
        for r in range(span):
            lat = 2 * p * rows - REACH + r
            if 0 <= lat < lats:
                pick[p * pitch + r, (lat % rows) * blocks + lat // rows] = 1
    return pick.astype(BF)


def on_device(
    grid_state,
    row_query,
    row_keyval,
    row_output,
    column_query,
    column_keyval,
    column_output,
    conv_kernel,
    gate_up,
    down_proj,
):
    rows, cols, width = grid_state.shape
    n = lax.axis_size("lon")
    m = lax.axis_size("lat")
    lons = cols // m
    padded = jnp.pad(grid_state, ((0, n - rows), (0, 0), (0, 0)))
    lines = lax.all_to_all(padded, "lon", 0, 0, tiled=True).reshape(n * cols, width)
    after_rows = row_attention(lines, row_query, row_keyval, row_output)
    moved = lax.all_to_all(after_rows.reshape(n * m, 2 * lons, 128), ("lon", "lat"), 0, 0, tiled=True)
    moved = moved.reshape(-1, 128)
    pick = jnp.asarray(selection(rows * m, rows))
    span = 2 * rows + 2 * REACH
    sent = column_attention(moved, column_query, column_keyval, column_output, pick, lons, span, m)
    own = lax.all_to_all(sent, "lat", 0, 0, tiled=True)
    k = HALO // lons
    left = lax.ppermute(own[m - k :], "lon", [(i, (i + 1) % n) for i in range(n)])
    right = lax.ppermute(own[:k], "lon", [((i + 1) % n, i) for i in range(n)])
    taps = jnp.swapaxes(conv_kernel, 0, 1)
    edge, mid, done = inner_levels(own, taps, rows * m, rows)
    keep, send = outer_levels(left, right, edge, mid, done, taps, rows * m, rows, cols)
    got = lax.ppermute(send, "lat", [(i, i ^ 1) for i in range(m)])
    return feed_forward(keep, got, gate_up, down_proj)


def solution(mesh):
    return jax.shard_map(
        on_device,
        mesh=mesh,
        in_specs=(P("lat", "lon", None), P(), P(), P(), P(), P(), P(), P(), P(), P()),
        out_specs=P("lat", "lon", None),
        check_vma=False,
    )
```

```python
import functools
import jax
import jax.numpy as jnp
import numpy as np
from jax import lax
from jax.sharding import PartitionSpec as P
from jax.experimental import pallas as pl
from jax.experimental.pallas import tpu as pltpu

BF = jnp.bfloat16
F32 = jnp.float32
HEADS = 8
NT = (((1,), (1,)), ((), ()))
SCALE = 1.4426950408889634 * 32**-0.5
VMEM = pl.BlockSpec(memory_space=pltpu.VMEM)
LIMIT = 24 * 2**20


def norm(values):
    values = values.astype(F32)
    center = values - jnp.mean(values, -1, keepdims=True)
    spread = jnp.mean(center * center, -1, keepdims=True)
    return (center * lax.rsqrt(spread + 1e-5)).astype(BF)


def mm(a, b):
    return jnp.dot(a, b, preferred_element_type=F32)


def value_rows(values):
    turned = jnp.transpose(values)
    one = jnp.ones((16, values.shape[0]), BF)
    return [jnp.concatenate([turned[32 * h : 32 * h + 32], one], 0) for h in range(HEADS)]


def attend(q, keys, value_of, pieces=2):
    lane = lax.broadcasted_iota(jnp.int32, (1, 256), 1) >> 5
    size = q.shape[0] // pieces

    def scores_of(h, z):
        some = q[z * size : z * size + size]
        masked = jnp.where(lane == h, some, jnp.zeros_like(some))
        return lax.dot_general(keys, masked, NT, preferred_element_type=F32)

    order = [(h, z) for h in range(HEADS) for z in range(pieces)]
    parts = [[] for _ in range(pieces)]
    later = scores_of(*order[0])
    for at, (h, z) in enumerate(order):
        scores = later
        if at + 1 < len(order):
            later = scores_of(*order[at + 1])
        highest = jnp.max(scores, 0, keepdims=True)
        weights = jnp.exp2((scores - highest) * SCALE).astype(BF)
        sums = mm(value_of(h), weights)
        parts[z].append(sums[:32] / sums[32:33])
    whole = jnp.concatenate([jnp.concatenate(p, 0) for p in parts], 1)
    return jnp.transpose(whole).astype(BF)


def value_blocks(values):
    lane = lax.broadcasted_iota(jnp.int32, (1, 128), 1) >> 5
    one = jnp.ones((values.shape[0], 128), BF)
    blocks = []
    for h in range(HEADS):
        group = values[:, 128 * (h // 4) : 128 * (h // 4) + 128]
        blocks.append(jnp.concatenate([jnp.where(lane == h % 4, group, jnp.zeros_like(group)), one], -1))
    return blocks


def attend_short(q, keys, values):
    lane = lax.broadcasted_iota(jnp.int32, (1, 256), 1) >> 5
    blocks = value_blocks(values)

    def scores_of(h):
        masked = jnp.where(lane == h, q, jnp.zeros_like(q))
        return lax.dot_general(masked, keys, NT, preferred_element_type=F32)

    halves = []
    later = scores_of(0)
    for g in range(2):
        total = None
        for h in range(4 * g, 4 * g + 4):
            scores = later
            if h + 1 < HEADS:
                later = scores_of(h + 1)
            highest = jnp.max(scores, -1, keepdims=True)
            weights = jnp.exp2((scores - highest) * SCALE).astype(BF)
            sums = mm(weights, blocks[h])
            part = sums[:, :128] / sums[:, 128:]
            total = part if total is None else total + part
        halves.append(total.astype(BF))
    return jnp.concatenate(halves, -1)


def row_kernel(qb, x_ref, wq_ref, wkv_ref, wo_ref, o_ref, q_s, k_s, v_s, o_s):
    rows = x_ref.shape[0]
    n = norm(x_ref[...])
    q_s[...] = mm(n, wq_ref[...]).astype(BF)
    kv = mm(n, wkv_ref[...]).astype(BF)
    k_s[...] = kv[:, :256]
    for h, block in enumerate(value_rows(kv[:, 256:])):
        v_s[h] = block

    def body(i, _):
        sl = pl.ds(pl.multiple_of(i * qb, qb), qb)
        mixed = attend(q_s[sl, :], k_s[...], lambda h: v_s[h])
        after = x_ref[sl, :].astype(F32) + mm(mixed, wo_ref[...])
        for hf in range(2):
            o_s[pl.ds(hf, qb, 2), :] = after[:, hf * 128 : hf * 128 + 128]
        o_ref[pl.ds(pl.multiple_of(i * 2 * qb, 2 * qb), 2 * qb), :] = o_s[...].astype(BF)
        return 0

    lax.fori_loop(0, rows // qb, body, 0)


def row_attention(x, wq, wkv, wo, qb=1024):
    rows = x.shape[0]
    return pl.pallas_call(
        functools.partial(row_kernel, qb),
        out_shape=jax.ShapeDtypeStruct((2 * rows, 128), BF),
        in_specs=[VMEM] * 4,
        out_specs=VMEM,
        scratch_shapes=[
            pltpu.VMEM((rows, 256), BF),
            pltpu.VMEM((rows, 256), BF),
            pltpu.VMEM((HEADS, 48, rows), BF),
            pltpu.VMEM((2 * qb, 128), F32),
        ],
        compiler_params=pltpu.CompilerParams(vmem_limit_bytes=LIMIT),
        name="row_attention",
    )(x, wq, wkv, wo)


def column_kernel(lons, span, unroll, x_ref, wq_ref, wkv_ref, wo_ref, sel_ref, o_ref, x_s, o_s):
    step = 2 * lons
    lats = sel_ref.shape[1]
    x_s[...] = x_ref[: lats * step].astype(F32)
    size = lons * span
    blocks = o_ref.shape[0] // 2
    pitch = sel_ref.shape[0] // blocks

    def body(b, _):
        x = jnp.concatenate([x_s[pl.ds(2 * b + hf, lats, step), :] for hf in range(2)], -1)
        n = norm(x)
        q = mm(n, wq_ref[...]).astype(BF)
        kv = mm(n, wkv_ref[...]).astype(BF)
        mixed = attend_short(q, kv[:, :256], kv[:, 256:])
        after = (x + mm(mixed, wo_ref[...])).astype(BF)
        sent = mm(sel_ref[...], after)
        for p in range(blocks):
            for hf in range(2):
                part = sent[p * pitch : p * pitch + span, hf * 128 : hf * 128 + 128]
                o_s[hf, pl.ds(p * size + b * span, span), :] = part
        return 0

    if unroll == lons:
        for b in range(lons):
            body(b, 0)
    else:
        lax.fori_loop(0, lons, body, 0, unroll=unroll)
    for p in range(o_ref.shape[0]):
        o_ref[p] = o_s[p // blocks, p % blocks * size : (p % blocks + 1) * size].astype(BF)


def column_attention(x, wq, wkv, wo, select, lons, span, peers, unroll=4):
    size = lons * span
    return pl.pallas_call(
        functools.partial(column_kernel, lons, span, unroll),
        out_shape=jax.ShapeDtypeStruct((peers, size, 128), BF),
        in_specs=[VMEM] * 5,
        out_specs=VMEM,
        scratch_shapes=[
            pltpu.VMEM((select.shape[1] * 2 * lons, 128), F32),
            pltpu.VMEM((2, peers // 2 * size, 128), F32),
        ],
        compiler_params=pltpu.CompilerParams(vmem_limit_bytes=LIMIT),
        name="column_attention",
    )(x, wq, wkv, wo, select)


REACH = 15
U_IN, U_OUT, U_LAST = 4, 4, 7
S = 8
HALO = 16


ROOT_HALF = 0.7071067811865476


def taps_of(w_ref, level, half):
    out = []
    for k in range(9):
        both = w_ref[k, level : level + 1, :]
        mine = jnp.where(half == 0, both[:, :128], both[:, 128:])
        out.append(jnp.broadcast_to(mine * ROOT_HALF, (S, 128)))
    return out


def convolved(src, width, taps, i, at, rate):
    def cell(a, b):
        return src[pl.ds((i + (a - 1) * rate) * width + at + (b - 1) * rate, S), :]

    lines = []
    for a in range(3):
        terms = [taps[3 * a + b] * cell(a, b) for b in range(3)]
        lines.append(terms[0] + terms[1] + terms[2])
    total = lines[0] + lines[1] + lines[2]
    part = ROOT_HALF * total
    return (cell(1, 1) + part + part * lax.erf(total)).astype(BF)


def spread(part, buf, width, lon, rows):
    values = part.astype(F32)
    for b in range(part.shape[0] // rows):
        at = 0
        while at < rows:
            place = b * rows + at
            count = min(rows - at, S - place % S)
            buf[pl.ds(at * width + lon + b, count, width), :] = values[place : place + count]
            at += count


def position(rows):
    return lax.axis_index("block") * (2 * rows) - REACH, lax.axis_index("half")


def clear_outside(first, rows0, lats, clear):
    def one(i, _):
        clear(i)
        return 0

    @pl.when(first < 0)
    def _():
        lax.fori_loop(0, REACH, one, 0)

    @pl.when(first + rows0 > lats)
    def _():
        lax.fori_loop(rows0 - REACH, rows0, one, 0)


INNER = ((17, 25, 33, 41, 49, 57, 65, 71), (19, 27, 35, 43, 51, 59, 67, 69), (23, 31, 39, 47, 55, 63, 65))
MIDDLE = (2, 3, 4, 5)
OUTER = ((2, 9, 79, 86), (4, 11, 77, 84), (8, 15, 73, 80))


def inner_kernel(lats, rows, own_ref, w_ref, edge_ref, mid_ref, done_ref, a_s, b_s):
    first, half = position(rows)
    rows0 = edge_ref.shape[1]
    width = own_ref.shape[0] * own_ref.shape[1] // rows0
    per = own_ref.shape[1] // rows0
    for k in range(own_ref.shape[0]):
        spread(own_ref[k], a_s, width, k * per, rows0)

    def raw(i, _):
        ends = [a_s[pl.ds(i * width + c, S), :] for c in (0, width - S)]
        edge_ref[0, i] = jnp.concatenate(ends, 0).astype(BF)
        return 0

    lax.fori_loop(0, rows0, raw, 0, unroll=2)
    src, dst = a_s, b_s
    edge = 0
    for level in range(3):
        rate = 2**level
        edge += rate
        taps = taps_of(w_ref, level, half)

        def row(i, _, src=src, dst=dst, taps=taps, rate=rate, edge=edge, level=level):
            i = i + edge
            out = [convolved(src, width, taps, i, c - HALO, rate) for c in INNER[level]]
            for c, v in zip(INNER[level], out):
                dst[pl.ds(i * width + c - HALO, S), :] = v.astype(F32)
            if level < 2:
                edge_ref[level + 1, i] = jnp.concatenate([out[0], out[-1]], 0)
            else:
                mid_ref[i - edge] = jnp.concatenate(out, 0)
            return 0

        lax.fori_loop(0, rows0 - 2 * edge, row, 0, unroll=U_IN)

        def clear(i, dst=dst):
            for c in range(0, width, S):
                dst[pl.ds(i * width + c, S), :] = jnp.zeros((S, 128), F32)

        clear_outside(first, rows0, lats, clear)
        src, dst = dst, src

    taps = taps_of(w_ref, 3, half)

    def last(i, _):
        out = [convolved(src, width, taps, i + REACH, q * S, 8) for q in MIDDLE]
        done_ref[i] = jnp.concatenate(out, 0)
        return 0

    lax.fori_loop(0, 2 * rows, last, 0, unroll=U_LAST)


def inner_levels(own, taps, lats, rows):
    rows0 = 2 * rows + 2 * REACH
    per = own.shape[0] * own.shape[1]
    return pl.pallas_call(
        functools.partial(inner_kernel, lats, rows),
        out_shape=(
            jax.ShapeDtypeStruct((3, rows0, 2 * S, 128), BF),
            jax.ShapeDtypeStruct((rows0 - 14, len(INNER[2]) * S, 128), BF),
            jax.ShapeDtypeStruct((2 * rows, len(MIDDLE) * S, 128), BF),
        ),
        in_specs=[VMEM] * 2,
        out_specs=(VMEM, VMEM, VMEM),
        scratch_shapes=[pltpu.VMEM((per, 128), F32)] * 2,
        compiler_params=pltpu.CompilerParams(vmem_limit_bytes=LIMIT),
        cost_estimate=pl.CostEstimate(flops=60000000, bytes_accessed=8000000, transcendentals=1000000),
        name="inner_levels",
    )(own, taps)


def outer_kernel(lats, left_ref, right_ref, edge_ref, mid_ref, done_ref, w_ref, keep_ref, send_ref, *bufs):
    rows, cols, _ = keep_ref.shape
    first, half = position(rows)
    rows0 = edge_ref.shape[1]
    width = cols + 2 * HALO
    per = left_ref.shape[1] // rows0
    for k in range(left_ref.shape[0]):
        spread(left_ref[k], bufs[0], width, k * per, rows0)
        spread(right_ref[k], bufs[0], width, HALO + cols + k * per, rows0)

    def ends(i, _):
        for level in range(3):
            at = (HALO, HALO + cols - S) if level == 0 else (INNER[level - 1][0], INNER[level - 1][-1])
            both = edge_ref[level, i].astype(F32)
            for e in range(2):
                bufs[level][pl.ds(i * width + at[e], S), :] = both[e * S : e * S + S]
        return 0

    lax.fori_loop(0, rows0, ends, 0, unroll=2)

    def middle(i, _):
        cells = mid_ref[i].astype(F32)
        for g, c in enumerate(INNER[2]):
            bufs[3][pl.ds((i + 7) * width + c, S), :] = cells[g * S : g * S + S]
        return 0

    lax.fori_loop(0, mid_ref.shape[0], middle, 0, unroll=4)
    edge = 0
    for level in range(3):
        rate = 2**level
        edge += rate
        taps = taps_of(w_ref, level, half)

        def row(i, _, taps=taps, rate=rate, edge=edge, level=level):
            i = i + edge
            out = [convolved(bufs[level], width, taps, i, c, rate) for c in OUTER[level]]
            for c, v in zip(OUTER[level], out):
                bufs[level + 1][pl.ds(i * width + c, S), :] = v.astype(F32)
            return 0

        lax.fori_loop(0, rows0 - 2 * edge, row, 0, unroll=U_OUT)

        def clear(i, level=level):
            for c in range(0, width, S):
                bufs[level + 1][pl.ds(i * width + c, S), :] = jnp.zeros((S, 128), F32)

        clear_outside(first, rows0, lats, clear)

    taps = taps_of(w_ref, 3, half)
    for ref, base in ((send_ref, (1 - half) * rows), (keep_ref, half * rows)):

        def last(i, _, ref=ref, base=base):
            row = base + REACH + i
            out = [
                done_ref[base + i] if q == MIDDLE[0] else convolved(bufs[3], width, taps, row, HALO + q * S, 8)
                for q in range(cols // S)
                if q not in MIDDLE[1:]
            ]
            ref[i] = jnp.concatenate(out, 0)
            return 0

        lax.fori_loop(0, rows, last, 0, unroll=U_LAST)


def outer_levels(left, right, edge, mid, done, taps, lats, rows, cols):
    rows0 = edge.shape[1]
    shape = jax.ShapeDtypeStruct((rows, cols, 128), BF)
    return pl.pallas_call(
        functools.partial(outer_kernel, lats),
        out_shape=(shape, shape),
        in_specs=[VMEM] * 6,
        out_specs=(VMEM, VMEM),
        scratch_shapes=[pltpu.VMEM((rows0 * (cols + 2 * HALO), 128), F32)] * 4,
        compiler_params=pltpu.CompilerParams(vmem_limit_bytes=LIMIT),
        cost_estimate=pl.CostEstimate(flops=40000000, bytes_accessed=4000000, transcendentals=500000),
        name="outer_levels",
    )(left, right, edge, mid, done, taps)


def feed_kernel(batch, keep_ref, got_ref, gu_ref, down_ref, o_ref):
    rows, cols, _ = keep_ref.shape
    half = lax.axis_index("half")

    def feed(c, _):
        sl = pl.ds(c * batch, batch)
        keep = keep_ref[sl].reshape(batch * cols, 128)
        got = got_ref[sl].reshape(batch * cols, 128)
        state = jnp.concatenate(
            [jnp.where(half == 0, keep, got), jnp.where(half == 0, got, keep)], -1
        ).astype(F32)
        both = mm(norm(state), gu_ref[...])
        units = gu_ref.shape[1] // 2
        gate, up = both[:, :units], both[:, units:]
        hidden = (gate / (1.0 + jnp.exp(-gate)) * up).astype(BF)
        out = (state + mm(hidden, down_ref[...])).astype(BF)
        o_ref[sl] = out.reshape(batch, cols, 256)
        return 0

    lax.fori_loop(0, rows // batch, feed, 0)


def feed_forward(keep, got, gate_up, down, batch=14):
    rows, cols, _ = keep.shape
    return pl.pallas_call(
        functools.partial(feed_kernel, batch),
        out_shape=jax.ShapeDtypeStruct((rows, cols, 256), BF),
        in_specs=[VMEM] * 4,
        out_specs=VMEM,
        compiler_params=pltpu.CompilerParams(vmem_limit_bytes=LIMIT),
        name="feed_forward",
    )(keep, got, gate_up, down)


def selection(lats, rows):
    blocks = lats // rows
    span = 2 * rows + 2 * REACH
    pitch = -(-span // 16) * 16
    pick = np.zeros((blocks // 2 * pitch, lats), np.float32)
    for p in range(blocks // 2):
        for r in range(span):
            lat = 2 * p * rows - REACH + r
            if 0 <= lat < lats:
                at = lat // rows
                pick[p * pitch + r, (lat % rows) * blocks + at % 2 * (blocks // 2) + at // 2] = 1
    return pick.astype(BF)


def on_device(
    grid_state,
    row_query,
    row_keyval,
    row_output,
    column_query,
    column_keyval,
    column_output,
    conv_kernel,
    gate_up,
    down_proj,
):
    rows, cols, width = grid_state.shape
    n = lax.axis_size("lon")
    m = 2 * lax.axis_size("block")
    lat = ("half", "block")
    lons = cols // m
    padded = jnp.pad(grid_state, ((0, n - rows), (0, 0), (0, 0)))
    lines = lax.all_to_all(padded, "lon", 0, 0, tiled=True).reshape(n * cols, width)
    after_rows = row_attention(lines, row_query, row_keyval, row_output)
    moved = lax.all_to_all(after_rows.reshape(n * m, 2 * lons, 128), ("lon",) + lat, 0, 0, tiled=True)
    moved = moved.reshape(-1, 128)
    pick = jnp.asarray(selection(rows * m, rows))
    span = 2 * rows + 2 * REACH
    sent = column_attention(moved, column_query, column_keyval, column_output, pick, lons, span, m)
    own = lax.all_to_all(sent, lat, 0, 0, tiled=True)
    k = HALO // lons
    left = lax.ppermute(own[m - k :], "lon", [(i, (i + 1) % n) for i in range(n)])
    right = lax.ppermute(own[:k], "lon", [((i + 1) % n, i) for i in range(n)])
    taps = jnp.swapaxes(conv_kernel, 0, 1)
    edge, mid, done = inner_levels(own, taps, rows * m, rows)
    keep, send = outer_levels(left, right, edge, mid, done, taps, rows * m, rows, cols)
    got = lax.ppermute(send, "half", [(0, 1), (1, 0)])
    return feed_forward(keep, got, gate_up, down_proj)


def solution(mesh):
    n, m = mesh.devices.shape
    pairs = jax.sharding.Mesh(mesh.devices.reshape(n, m // 2, 2), ("lon", "block", "half"))
    cells = P(("block", "half"), "lon", None)
    return jax.shard_map(
        on_device,
        mesh=pairs,
        in_specs=(cells, P(), P(), P(), P(), P(), P(), P(), P(), P()),
        out_specs=cells,
        check_vma=False,
    )
```

```python
import functools
import jax
import jax.numpy as jnp
import numpy as np
from jax import lax
from jax.sharding import PartitionSpec as P
from jax.experimental import pallas as pl
from jax.experimental.pallas import tpu as pltpu

BF = jnp.bfloat16
F32 = jnp.float32
HEADS = 8
NT = (((1,), (1,)), ((), ()))
SCALE = 1.4426950408889634 * 32**-0.5
VMEM = pl.BlockSpec(memory_space=pltpu.VMEM)
LIMIT = 24 * 2**20


def norm(values):
    values = values.astype(F32)
    center = values - jnp.mean(values, -1, keepdims=True)
    spread = jnp.mean(center * center, -1, keepdims=True)
    return (center * lax.rsqrt(spread + 1e-5)).astype(BF)


def mm(a, b):
    return jnp.dot(a, b, preferred_element_type=F32)


def value_rows(values):
    turned = jnp.transpose(values)
    one = jnp.ones((16, values.shape[0]), BF)
    return [jnp.concatenate([turned[32 * h : 32 * h + 32], one], 0) for h in range(HEADS)]


def attend(q, keys, value_of, pieces=2):
    lane = lax.broadcasted_iota(jnp.int32, (1, 256), 1) >> 5
    size = q.shape[0] // pieces

    def scores_of(h, z):
        some = q[z * size : z * size + size]
        masked = jnp.where(lane == h, some, jnp.zeros_like(some))
        return lax.dot_general(keys, masked, NT, preferred_element_type=F32)

    order = [(h, z) for h in range(HEADS) for z in range(pieces)]
    parts = [[] for _ in range(pieces)]
    later = scores_of(*order[0])
    for at, (h, z) in enumerate(order):
        scores = later
        if at + 1 < len(order):
            later = scores_of(*order[at + 1])
        highest = jnp.max(scores, 0, keepdims=True)
        weights = jnp.exp2((scores - highest) * SCALE).astype(BF)
        sums = mm(value_of(h), weights)
        parts[z].append(sums[:32] / sums[32:33])
    whole = jnp.concatenate([jnp.concatenate(p, 0) for p in parts], 1)
    return jnp.transpose(whole).astype(BF)


def value_blocks(values):
    lane = lax.broadcasted_iota(jnp.int32, (1, 128), 1) >> 5
    one = jnp.ones((values.shape[0], 128), BF)
    blocks = []
    for h in range(HEADS):
        group = values[:, 128 * (h // 4) : 128 * (h // 4) + 128]
        blocks.append(jnp.concatenate([jnp.where(lane == h % 4, group, jnp.zeros_like(group)), one], -1))
    return blocks


def attend_short(q, keys, values):
    lane = lax.broadcasted_iota(jnp.int32, (1, 256), 1) >> 5
    blocks = value_blocks(values)

    def scores_of(h):
        masked = jnp.where(lane == h, q, jnp.zeros_like(q))
        return lax.dot_general(masked, keys, NT, preferred_element_type=F32)

    halves = []
    later = scores_of(0)
    for g in range(2):
        total = None
        for h in range(4 * g, 4 * g + 4):
            scores = later
            if h + 1 < HEADS:
                later = scores_of(h + 1)
            highest = jnp.max(scores, -1, keepdims=True)
            weights = jnp.exp2((scores - highest) * SCALE).astype(BF)
            sums = mm(weights, blocks[h])
            part = sums[:, :128] / sums[:, 128:]
            total = part if total is None else total + part
        halves.append(total.astype(BF))
    return jnp.concatenate(halves, -1)


def row_kernel(qb, x_ref, wq_ref, wkv_ref, wo_ref, o_ref, q_s, k_s, v_s, o_s):
    rows = x_ref.shape[0]
    n = norm(x_ref[...])
    q_s[...] = mm(n, wq_ref[...]).astype(BF)
    kv = mm(n, wkv_ref[...]).astype(BF)
    k_s[...] = kv[:, :256]
    for h, block in enumerate(value_rows(kv[:, 256:])):
        v_s[h] = block

    def body(i, _):
        sl = pl.ds(pl.multiple_of(i * qb, qb), qb)
        mixed = attend(q_s[sl, :], k_s[...], lambda h: v_s[h])
        after = x_ref[sl, :].astype(F32) + mm(mixed, wo_ref[...])
        for hf in range(2):
            o_s[pl.ds(hf, qb, 2), :] = after[:, hf * 128 : hf * 128 + 128]
        o_ref[pl.ds(pl.multiple_of(i * 2 * qb, 2 * qb), 2 * qb), :] = o_s[...].astype(BF)
        return 0

    lax.fori_loop(0, rows // qb, body, 0)


def row_attention(x, wq, wkv, wo, qb=1024):
    rows = x.shape[0]
    return pl.pallas_call(
        functools.partial(row_kernel, qb),
        out_shape=jax.ShapeDtypeStruct((2 * rows, 128), BF),
        in_specs=[VMEM] * 4,
        out_specs=VMEM,
        scratch_shapes=[
            pltpu.VMEM((rows, 256), BF),
            pltpu.VMEM((rows, 256), BF),
            pltpu.VMEM((HEADS, 48, rows), BF),
            pltpu.VMEM((2 * qb, 128), F32),
        ],
        compiler_params=pltpu.CompilerParams(vmem_limit_bytes=LIMIT),
        name="row_attention",
    )(x, wq, wkv, wo)


def column_kernel(lons, span, unroll, x_ref, wq_ref, wkv_ref, wo_ref, sel_ref, o_ref, x_s, o_s):
    step = 2 * lons
    lats = sel_ref.shape[1]
    x_s[...] = x_ref[: lats * step].astype(F32)
    size = lons * span
    blocks = o_ref.shape[0] // 2
    pitch = sel_ref.shape[0] // blocks

    def body(b, _):
        x = jnp.concatenate([x_s[pl.ds(2 * b + hf, lats, step), :] for hf in range(2)], -1)
        n = norm(x)
        q = mm(n, wq_ref[...]).astype(BF)
        kv = mm(n, wkv_ref[...]).astype(BF)
        mixed = attend_short(q, kv[:, :256], kv[:, 256:])
        after = (x + mm(mixed, wo_ref[...])).astype(BF)
        sent = mm(sel_ref[...], after)
        for p in range(blocks):
            for hf in range(2):
                part = sent[p * pitch : p * pitch + span, hf * 128 : hf * 128 + 128]
                o_s[hf, pl.ds(p * size + b * span, span), :] = part
        return 0

    if unroll == lons:
        for b in range(lons):
            body(b, 0)
    else:
        lax.fori_loop(0, lons, body, 0, unroll=unroll)
    for p in range(o_ref.shape[0]):
        o_ref[p] = o_s[p // blocks, p % blocks * size : (p % blocks + 1) * size].astype(BF)


def column_attention(x, wq, wkv, wo, select, lons, span, peers, unroll=4):
    size = lons * span
    return pl.pallas_call(
        functools.partial(column_kernel, lons, span, unroll),
        out_shape=jax.ShapeDtypeStruct((peers, size, 128), BF),
        in_specs=[VMEM] * 5,
        out_specs=VMEM,
        scratch_shapes=[
            pltpu.VMEM((select.shape[1] * 2 * lons, 128), F32),
            pltpu.VMEM((2, peers // 2 * size, 128), F32),
        ],
        compiler_params=pltpu.CompilerParams(vmem_limit_bytes=LIMIT),
        name="column_attention",
    )(x, wq, wkv, wo, select)


REACH = 15
U_IN, U_OUT, U_LAST = 4, 4, 7
S = 8
HALO = 16


ROOT_HALF = 0.7071067811865476


def taps_of(w_ref, level, half):
    out = []
    for k in range(9):
        both = w_ref[k, level : level + 1, :]
        mine = jnp.where(half == 0, both[:, :128], both[:, 128:])
        out.append(jnp.broadcast_to(mine * ROOT_HALF, (S, 128)))
    return out


def convolved(src, width, taps, i, at, rate):
    def cell(a, b):
        return src[pl.ds((i + (a - 1) * rate) * width + at + (b - 1) * rate, S), :]

    lines = []
    for a in range(3):
        terms = [taps[3 * a + b] * cell(a, b) for b in range(3)]
        lines.append(terms[0] + terms[1] + terms[2])
    total = lines[0] + lines[1] + lines[2]
    part = ROOT_HALF * total
    return (cell(1, 1) + part + part * lax.erf(total)).astype(BF)


def spread(part, buf, width, lon, rows):
    values = part.astype(F32)
    for b in range(part.shape[0] // rows):
        at = 0
        while at < rows:
            place = b * rows + at
            count = min(rows - at, S - place % S)
            buf[pl.ds(at * width + lon + b, count, width), :] = values[place : place + count]
            at += count


def position(rows):
    return lax.axis_index("block") * (2 * rows) - REACH, lax.axis_index("half")


def clear_outside(first, rows0, lats, clear):
    def one(i, _):
        clear(i)
        return 0

    @pl.when(first < 0)
    def _():
        lax.fori_loop(0, REACH, one, 0)

    @pl.when(first + rows0 > lats)
    def _():
        lax.fori_loop(rows0 - REACH, rows0, one, 0)


INNER = ((17, 25, 33, 41, 49, 57, 65, 71), (19, 27, 35, 43, 51, 59, 67, 69), (23, 31, 39, 47, 55, 63, 65))
MIDDLE = (2, 3, 4, 5)
OUTER = ((2, 9, 79, 86), (4, 11, 77, 84), (8, 15, 73, 80))


def inner_kernel(lats, rows, own_ref, w_ref, edge_ref, mid_ref, done_ref, a_s, b_s):
    first, half = position(rows)
    rows0 = edge_ref.shape[1]
    width = own_ref.shape[0] * own_ref.shape[1] // rows0
    per = own_ref.shape[1] // rows0
    for k in range(own_ref.shape[0]):
        spread(own_ref[k], a_s, width, k * per, rows0)

    def raw(i, _):
        ends = [a_s[pl.ds(i * width + c, S), :] for c in (0, width - S)]
        edge_ref[0, i] = jnp.concatenate(ends, 0).astype(BF)
        return 0

    lax.fori_loop(0, rows0, raw, 0, unroll=2)
    src, dst = a_s, b_s
    edge = 0
    for level in range(3):
        rate = 2**level
        edge += rate
        taps = taps_of(w_ref, level, half)

        def row(i, _, src=src, dst=dst, taps=taps, rate=rate, edge=edge, level=level):
            i = i + edge
            out = [convolved(src, width, taps, i, c - HALO, rate) for c in INNER[level]]
            for c, v in zip(INNER[level], out):
                dst[pl.ds(i * width + c - HALO, S), :] = v.astype(F32)
            if level < 2:
                edge_ref[level + 1, i] = jnp.concatenate([out[0], out[-1]], 0)
            else:
                mid_ref[i - edge] = jnp.concatenate(out, 0)
            return 0

        lax.fori_loop(0, rows0 - 2 * edge, row, 0, unroll=U_IN)

        def clear(i, dst=dst):
            for c in range(0, width, S):
                dst[pl.ds(i * width + c, S), :] = jnp.zeros((S, 128), F32)

        clear_outside(first, rows0, lats, clear)
        src, dst = dst, src

    taps = taps_of(w_ref, 3, half)

    def last(i, _):
        out = [convolved(src, width, taps, i + REACH, q * S, 8) for q in MIDDLE]
        done_ref[i] = jnp.concatenate(out, 0)
        return 0

    lax.fori_loop(0, 2 * rows, last, 0, unroll=U_LAST)


def inner_levels(own, taps, lats, rows):
    rows0 = 2 * rows + 2 * REACH
    per = own.shape[0] * own.shape[1]
    return pl.pallas_call(
        functools.partial(inner_kernel, lats, rows),
        out_shape=(
            jax.ShapeDtypeStruct((3, rows0, 2 * S, 128), BF),
            jax.ShapeDtypeStruct((rows0 - 14, len(INNER[2]) * S, 128), BF),
            jax.ShapeDtypeStruct((2 * rows, len(MIDDLE) * S, 128), BF),
        ),
        in_specs=[VMEM] * 2,
        out_specs=(VMEM, VMEM, VMEM),
        scratch_shapes=[pltpu.VMEM((per, 128), F32)] * 2,
        compiler_params=pltpu.CompilerParams(vmem_limit_bytes=LIMIT),
        cost_estimate=pl.CostEstimate(flops=60000000, bytes_accessed=8000000, transcendentals=1000000),
        name="inner_levels",
    )(own, taps)


def outer_kernel(lats, left_ref, right_ref, edge_ref, mid_ref, done_ref, w_ref, keep_ref, near_ref, far_ref, *bufs):
    rows, cols, _ = keep_ref.shape
    first, half = position(rows)
    rows0 = edge_ref.shape[1]
    width = cols + 2 * HALO
    per = left_ref.shape[1] // rows0
    for k in range(left_ref.shape[0]):
        spread(left_ref[k], bufs[0], width, k * per, rows0)
        spread(right_ref[k], bufs[0], width, HALO + cols + k * per, rows0)

    def ends(i, _):
        for level in range(3):
            at = (HALO, HALO + cols - S) if level == 0 else (INNER[level - 1][0], INNER[level - 1][-1])
            both = edge_ref[level, i].astype(F32)
            for e in range(2):
                bufs[level][pl.ds(i * width + at[e], S), :] = both[e * S : e * S + S]
        return 0

    lax.fori_loop(0, rows0, ends, 0, unroll=2)

    def middle(i, _):
        cells = mid_ref[i].astype(F32)
        for g, c in enumerate(INNER[2]):
            bufs[3][pl.ds((i + 7) * width + c, S), :] = cells[g * S : g * S + S]
        return 0

    lax.fori_loop(0, mid_ref.shape[0], middle, 0, unroll=4)
    edge = 0
    for level in range(3):
        rate = 2**level
        edge += rate
        taps = taps_of(w_ref, level, half)

        def row(i, _, taps=taps, rate=rate, edge=edge, level=level):
            i = i + edge
            out = [convolved(bufs[level], width, taps, i, c, rate) for c in OUTER[level]]
            for c, v in zip(OUTER[level], out):
                bufs[level + 1][pl.ds(i * width + c, S), :] = v.astype(F32)
            return 0

        lax.fori_loop(0, rows0 - 2 * edge, row, 0, unroll=U_OUT)

        def clear(i, level=level):
            for c in range(0, width, S):
                bufs[level + 1][pl.ds(i * width + c, S), :] = jnp.zeros((S, 128), F32)

        clear_outside(first, rows0, lats, clear)

    taps = taps_of(w_ref, 3, half)
    other = (1 - half) * rows
    for ref, base in ((near_ref, other), (far_ref, other + rows // 2), (keep_ref, half * rows)):

        def last(i, _, ref=ref, base=base):
            row = base + REACH + i
            out = [
                done_ref[base + i] if q == MIDDLE[0] else convolved(bufs[3], width, taps, row, HALO + q * S, 8)
                for q in range(cols // S)
                if q not in MIDDLE[1:]
            ]
            ref[i] = jnp.concatenate(out, 0)
            return 0

        lax.fori_loop(0, ref.shape[0], last, 0, unroll=U_LAST)


def outer_levels(left, right, edge, mid, done, taps, lats, rows, cols):
    rows0 = edge.shape[1]
    shapes = [jax.ShapeDtypeStruct((r, cols, 128), BF) for r in (rows, rows // 2, rows // 2)]
    return pl.pallas_call(
        functools.partial(outer_kernel, lats),
        out_shape=shapes,
        in_specs=[VMEM] * 6,
        out_specs=[VMEM] * 3,
        scratch_shapes=[pltpu.VMEM((rows0 * (cols + 2 * HALO), 128), F32)] * 4,
        compiler_params=pltpu.CompilerParams(vmem_limit_bytes=LIMIT),
        cost_estimate=pl.CostEstimate(flops=40000000, bytes_accessed=4000000, transcendentals=500000),
        name="outer_levels",
    )(left, right, edge, mid, done, taps)


def feed_kernel(part, keep_ref, got_ref, gu_ref, down_ref, *refs):
    o_ref, o_s, sem = refs[-3:]
    rows, cols, _ = got_ref.shape
    half = lax.axis_index("half")
    keep = keep_ref[part * rows : part * rows + rows].reshape(rows * cols, 128)
    got = got_ref[...].reshape(rows * cols, 128)
    state = jnp.concatenate([jnp.where(half == 0, keep, got), jnp.where(half == 0, got, keep)], -1).astype(F32)
    both = mm(norm(state), gu_ref[...])
    units = gu_ref.shape[1] // 2
    gate, up = both[:, :units], both[:, units:]
    hidden = (gate / (1.0 + jnp.exp(-gate)) * up).astype(BF)
    out = (state + mm(hidden, down_ref[...])).astype(BF)
    o_s[...] = out.reshape(rows, cols, 256)
    copy = pltpu.make_async_copy(o_s, o_ref.at[pl.ds(part * rows, rows)], sem)
    copy.start()
    copy.wait()


def feed_forward(part, keep, got, gate_up, down, before=None):
    anywhere = pl.BlockSpec(memory_space=pl.ANY)
    more = [] if before is None else [before]
    return pl.pallas_call(
        functools.partial(feed_kernel, part),
        out_shape=jax.ShapeDtypeStruct(keep.shape[:2] + (256,), BF),
        in_specs=[VMEM] * 4 + [anywhere] * len(more),
        out_specs=anywhere,
        scratch_shapes=[pltpu.VMEM(got.shape[:2] + (256,), BF), pltpu.SemaphoreType.DMA],
        input_output_aliases={4: 0} if more else {},
        compiler_params=pltpu.CompilerParams(vmem_limit_bytes=LIMIT),
        cost_estimate=pl.CostEstimate(flops=700000000, bytes_accessed=2000000, transcendentals=500000),
        name="feed_forward",
    )(keep, got, gate_up, down, *more)


def selection(lats, rows):
    blocks = lats // rows
    span = 2 * rows + 2 * REACH
    pitch = -(-span // 16) * 16
    pick = np.zeros((blocks // 2 * pitch, lats), np.float32)
    for p in range(blocks // 2):
        for r in range(span):
            lat = 2 * p * rows - REACH + r
            if 0 <= lat < lats:
                at = lat // rows
                pick[p * pitch + r, (lat % rows) * blocks + at % 2 * (blocks // 2) + at // 2] = 1
    return pick.astype(BF)


def on_device(
    grid_state,
    row_query,
    row_keyval,
    row_output,
    column_query,
    column_keyval,
    column_output,
    conv_kernel,
    gate_up,
    down_proj,
):
    rows, cols, width = grid_state.shape
    n = lax.axis_size("lon")
    m = 2 * lax.axis_size("block")
    lat = ("half", "block")
    lons = cols // m
    padded = jnp.pad(grid_state, ((0, n - rows), (0, 0), (0, 0)))
    lines = lax.all_to_all(padded, "lon", 0, 0, tiled=True).reshape(n * cols, width)
    after_rows = row_attention(lines, row_query, row_keyval, row_output)
    moved = lax.all_to_all(after_rows.reshape(n * m, 2 * lons, 128), ("lon",) + lat, 0, 0, tiled=True)
    moved = moved.reshape(-1, 128)
    pick = jnp.asarray(selection(rows * m, rows))
    span = 2 * rows + 2 * REACH
    sent = column_attention(moved, column_query, column_keyval, column_output, pick, lons, span, m)
    own = lax.all_to_all(sent, lat, 0, 0, tiled=True)
    k = HALO // lons
    left = lax.ppermute(own[m - k :], "lon", [(i, (i + 1) % n) for i in range(n)])
    right = lax.ppermute(own[:k], "lon", [((i + 1) % n, i) for i in range(n)])
    taps = jnp.swapaxes(conv_kernel, 0, 1)
    edge, mid, done = inner_levels(own, taps, rows * m, rows)
    keep, near, far = outer_levels(left, right, edge, mid, done, taps, rows * m, rows, cols)
    swap = [(0, 1), (1, 0)]
    got = [lax.ppermute(part, "half", swap) for part in (near, far)]
    out = feed_forward(0, keep, got[0], gate_up, down_proj)
    return feed_forward(1, keep, got[1], gate_up, down_proj, out)


def solution(mesh):
    n, m = mesh.devices.shape
    pairs = jax.sharding.Mesh(mesh.devices.reshape(n, m // 2, 2), ("lon", "block", "half"))
    cells = P(("block", "half"), "lon", None)
    return jax.shard_map(
        on_device,
        mesh=pairs,
        in_specs=(cells, P(), P(), P(), P(), P(), P(), P(), P(), P()),
        out_specs=cells,
        check_vma=False,
    )
```

```python
import functools
import jax
import jax.numpy as jnp
import numpy as np
from jax import lax
from jax.sharding import PartitionSpec as P
from jax.experimental import pallas as pl
from jax.experimental.pallas import tpu as pltpu

BF = jnp.bfloat16
F32 = jnp.float32
HEADS = 8
NT = (((1,), (1,)), ((), ()))
SCALE = 1.4426950408889634 * 32**-0.5
VMEM = pl.BlockSpec(memory_space=pltpu.VMEM)
LIMIT = 24 * 2**20


def norm(values):
    values = values.astype(F32)
    center = values - jnp.mean(values, -1, keepdims=True)
    spread = jnp.mean(center * center, -1, keepdims=True)
    return (center * lax.rsqrt(spread + 1e-5)).astype(BF)


def mm(a, b):
    return jnp.dot(a, b, preferred_element_type=F32)


def value_rows(values):
    turned = jnp.transpose(values)
    one = jnp.ones((16, values.shape[0]), BF)
    return [jnp.concatenate([turned[32 * h : 32 * h + 32], one], 0) for h in range(HEADS)]


def attend(q, keys, value_of, pieces=2):
    lane = lax.broadcasted_iota(jnp.int32, (1, 256), 1) >> 5
    size = q.shape[0] // pieces

    def scores_of(h, z):
        some = q[z * size : z * size + size]
        masked = jnp.where(lane == h, some, jnp.zeros_like(some))
        return lax.dot_general(keys, masked, NT, preferred_element_type=F32)

    order = [(h, z) for h in range(HEADS) for z in range(pieces)]
    parts = [[] for _ in range(pieces)]
    later = scores_of(*order[0])
    for at, (h, z) in enumerate(order):
        scores = later
        if at + 1 < len(order):
            later = scores_of(*order[at + 1])
        highest = jnp.max(scores, 0, keepdims=True)
        weights = jnp.exp2((scores - highest) * SCALE).astype(BF)
        sums = mm(value_of(h), weights)
        parts[z].append(sums[:32] / sums[32:33])
    whole = jnp.concatenate([jnp.concatenate(p, 0) for p in parts], 1)
    return jnp.transpose(whole).astype(BF)


def value_blocks(values):
    lane = lax.broadcasted_iota(jnp.int32, (1, 128), 1) >> 5
    one = jnp.ones((values.shape[0], 128), BF)
    blocks = []
    for h in range(HEADS):
        group = values[:, 128 * (h // 4) : 128 * (h // 4) + 128]
        blocks.append(jnp.concatenate([jnp.where(lane == h % 4, group, jnp.zeros_like(group)), one], -1))
    return blocks


def attend_short(q, keys, values):
    lane = lax.broadcasted_iota(jnp.int32, (1, 256), 1) >> 5
    blocks = value_blocks(values)

    def scores_of(h):
        masked = jnp.where(lane == h, q, jnp.zeros_like(q))
        return lax.dot_general(masked, keys, NT, preferred_element_type=F32)

    halves = []
    later = scores_of(0)
    for g in range(2):
        total = None
        for h in range(4 * g, 4 * g + 4):
            scores = later
            if h + 1 < HEADS:
                later = scores_of(h + 1)
            highest = jnp.max(scores, -1, keepdims=True)
            weights = jnp.exp2((scores - highest) * SCALE).astype(BF)
            sums = mm(weights, blocks[h])
            part = sums[:, :128] / sums[:, 128:]
            total = part if total is None else total + part
        halves.append(total.astype(BF))
    return jnp.concatenate(halves, -1)


def row_kernel(qb, x_ref, wq_ref, wkv_ref, wo_ref, o_ref, q_s, k_s, v_s, o_s):
    rows = x_ref.shape[0]
    n = norm(x_ref[...])
    q_s[...] = mm(n, wq_ref[...]).astype(BF)
    kv = mm(n, wkv_ref[...]).astype(BF)
    k_s[...] = kv[:, :256]
    for h, block in enumerate(value_rows(kv[:, 256:])):
        v_s[h] = block

    def body(i, _):
        sl = pl.ds(pl.multiple_of(i * qb, qb), qb)
        mixed = attend(q_s[sl, :], k_s[...], lambda h: v_s[h])
        after = x_ref[sl, :].astype(F32) + mm(mixed, wo_ref[...])
        for hf in range(2):
            o_s[pl.ds(hf, qb, 2), :] = after[:, hf * 128 : hf * 128 + 128]
        o_ref[pl.ds(pl.multiple_of(i * 2 * qb, 2 * qb), 2 * qb), :] = o_s[...].astype(BF)
        return 0

    lax.fori_loop(0, rows // qb, body, 0)


def row_attention(x, wq, wkv, wo, qb=1024):
    rows = x.shape[0]
    return pl.pallas_call(
        functools.partial(row_kernel, qb),
        out_shape=jax.ShapeDtypeStruct((2 * rows, 128), BF),
        in_specs=[VMEM] * 4,
        out_specs=VMEM,
        scratch_shapes=[
            pltpu.VMEM((rows, 256), BF),
            pltpu.VMEM((rows, 256), BF),
            pltpu.VMEM((HEADS, 48, rows), BF),
            pltpu.VMEM((2 * qb, 128), F32),
        ],
        compiler_params=pltpu.CompilerParams(vmem_limit_bytes=LIMIT),
        name="row_attention",
    )(x, wq, wkv, wo)


def column_kernel(lons, span, unroll, x_ref, wq_ref, wkv_ref, wo_ref, sel_ref, o_ref, x_s, o_s):
    step = 2 * lons
    lats = sel_ref.shape[1]
    x_s[...] = x_ref[: lats * step].astype(F32)
    size = lons * span
    blocks = o_ref.shape[0] // 2
    pitch = sel_ref.shape[0] // blocks

    def body(b, _):
        x = jnp.concatenate([x_s[pl.ds(2 * b + hf, lats, step), :] for hf in range(2)], -1)
        n = norm(x)
        q = mm(n, wq_ref[...]).astype(BF)
        kv = mm(n, wkv_ref[...]).astype(BF)
        mixed = attend_short(q, kv[:, :256], kv[:, 256:])
        after = (x + mm(mixed, wo_ref[...])).astype(BF)
        sent = mm(sel_ref[...], after)
        for p in range(blocks):
            for hf in range(2):
                part = sent[p * pitch : p * pitch + span, hf * 128 : hf * 128 + 128]
                o_s[hf, pl.ds(p * size + b * span, span), :] = part
        return 0

    if unroll == lons:
        for b in range(lons):
            body(b, 0)
    else:
        lax.fori_loop(0, lons, body, 0, unroll=unroll)
    for p in range(o_ref.shape[0]):
        o_ref[p] = o_s[p // blocks, p % blocks * size : (p % blocks + 1) * size].astype(BF)


def column_attention(x, wq, wkv, wo, select, lons, span, peers, unroll=4):
    size = lons * span
    return pl.pallas_call(
        functools.partial(column_kernel, lons, span, unroll),
        out_shape=jax.ShapeDtypeStruct((peers, size, 128), BF),
        in_specs=[VMEM] * 5,
        out_specs=VMEM,
        scratch_shapes=[
            pltpu.VMEM((select.shape[1] * 2 * lons, 128), F32),
            pltpu.VMEM((2, peers // 2 * size, 128), F32),
        ],
        compiler_params=pltpu.CompilerParams(vmem_limit_bytes=LIMIT),
        name="column_attention",
    )(x, wq, wkv, wo, select)


REACH = 15
U_IN, U_OUT, U_LAST = 4, 4, 7
S = 8
HALO = 16


ROOT_HALF = 0.7071067811865476


def taps_of(w_ref, level, half):
    out = []
    for k in range(9):
        both = w_ref[k, level : level + 1, :]
        mine = jnp.where(half == 0, both[:, :128], both[:, 128:])
        out.append(jnp.broadcast_to(mine * ROOT_HALF, (S, 128)))
    return out


def convolved(src, width, taps, i, at, rate):
    def cell(a, b):
        return src[pl.ds((i + (a - 1) * rate) * width + at + (b - 1) * rate, S), :]

    lines = []
    for a in range(3):
        terms = [taps[3 * a + b] * cell(a, b) for b in range(3)]
        lines.append(terms[0] + terms[1] + terms[2])
    total = lines[0] + lines[1] + lines[2]
    part = ROOT_HALF * total
    return (cell(1, 1) + (part + part * lax.erf(total))).astype(BF)


def spread(part, buf, width, lon, rows):
    values = part.astype(F32)
    for b in range(part.shape[0] // rows):
        at = 0
        while at < rows:
            place = b * rows + at
            count = min(rows - at, S - place % S)
            buf[pl.ds(at * width + lon + b, count, width), :] = values[place : place + count]
            at += count


def position(rows):
    return lax.axis_index("block") * (2 * rows) - REACH, lax.axis_index("half")


def clear_outside(first, rows0, lats, clear):
    def one(i, _):
        clear(i)
        return 0

    @pl.when(first < 0)
    def _():
        lax.fori_loop(0, REACH, one, 0)

    @pl.when(first + rows0 > lats)
    def _():
        lax.fori_loop(rows0 - REACH, rows0, one, 0)


INNER = ((17, 25, 33, 41, 49, 57, 65, 71), (19, 27, 35, 43, 51, 59, 67, 69), (23, 31, 39, 47, 55, 63, 65))
MIDDLE = (2, 3, 4, 5)
OUTER = ((2, 9, 79, 86), (4, 11, 77, 84), (8, 15, 73, 80))


def inner_kernel(lats, rows, own_ref, w_ref, edge_ref, mid_ref, done_ref, a_s, b_s):
    first, half = position(rows)
    rows0 = edge_ref.shape[1]
    width = own_ref.shape[0] * own_ref.shape[1] // rows0
    per = own_ref.shape[1] // rows0
    for k in range(own_ref.shape[0]):
        spread(own_ref[k], a_s, width, k * per, rows0)

    def raw(i, _):
        ends = [a_s[pl.ds(i * width + c, S), :] for c in (0, width - S)]
        edge_ref[0, i] = jnp.concatenate(ends, 0).astype(BF)
        return 0

    lax.fori_loop(0, rows0, raw, 0, unroll=2)
    src, dst = a_s, b_s
    edge = 0
    for level in range(3):
        rate = 2**level
        edge += rate
        taps = taps_of(w_ref, level, half)

        def row(i, _, src=src, dst=dst, taps=taps, rate=rate, edge=edge, level=level):
            i = i + edge
            out = [convolved(src, width, taps, i, c - HALO, rate) for c in INNER[level]]
            for c, v in zip(INNER[level], out):
                dst[pl.ds(i * width + c - HALO, S), :] = v.astype(F32)
            if level < 2:
                edge_ref[level + 1, i] = jnp.concatenate([out[0], out[-1]], 0)
            else:
                mid_ref[i - edge] = jnp.concatenate(out, 0)
            return 0

        lax.fori_loop(0, rows0 - 2 * edge, row, 0, unroll=U_IN)

        def clear(i, dst=dst):
            for c in range(0, width, S):
                dst[pl.ds(i * width + c, S), :] = jnp.zeros((S, 128), F32)

        clear_outside(first, rows0, lats, clear)
        src, dst = dst, src

    taps = taps_of(w_ref, 3, half)

    def last(i, _):
        out = [convolved(src, width, taps, i + REACH, q * S, 8) for q in MIDDLE]
        done_ref[i] = jnp.concatenate(out, 0)
        return 0

    lax.fori_loop(0, 2 * rows, last, 0, unroll=U_LAST)


def inner_levels(own, taps, lats, rows):
    rows0 = 2 * rows + 2 * REACH
    per = own.shape[0] * own.shape[1]
    return pl.pallas_call(
        functools.partial(inner_kernel, lats, rows),
        out_shape=(
            jax.ShapeDtypeStruct((3, rows0, 2 * S, 128), BF),
            jax.ShapeDtypeStruct((rows0 - 14, len(INNER[2]) * S, 128), BF),
            jax.ShapeDtypeStruct((2 * rows, len(MIDDLE) * S, 128), BF),
        ),
        in_specs=[VMEM] * 2,
        out_specs=(VMEM, VMEM, VMEM),
        scratch_shapes=[pltpu.VMEM((per, 128), F32)] * 2,
        compiler_params=pltpu.CompilerParams(vmem_limit_bytes=LIMIT),
        cost_estimate=pl.CostEstimate(flops=60000000, bytes_accessed=8000000, transcendentals=1000000),
        name="inner_levels",
    )(own, taps)


def outer_kernel(lats, left_ref, right_ref, edge_ref, mid_ref, done_ref, w_ref, keep_ref, near_ref, far_ref, *bufs):
    rows, cols, _ = keep_ref.shape
    first, half = position(rows)
    rows0 = edge_ref.shape[1]
    width = cols + 2 * HALO
    per = left_ref.shape[1] // rows0
    for k in range(left_ref.shape[0]):
        spread(left_ref[k], bufs[0], width, k * per, rows0)
        spread(right_ref[k], bufs[0], width, HALO + cols + k * per, rows0)

    def ends(i, _):
        for level in range(3):
            at = (HALO, HALO + cols - S) if level == 0 else (INNER[level - 1][0], INNER[level - 1][-1])
            both = edge_ref[level, i].astype(F32)
            for e in range(2):
                bufs[level][pl.ds(i * width + at[e], S), :] = both[e * S : e * S + S]
        return 0

    lax.fori_loop(0, rows0, ends, 0, unroll=2)

    def middle(i, _):
        cells = mid_ref[i].astype(F32)
        for g, c in enumerate(INNER[2]):
            bufs[3][pl.ds((i + 7) * width + c, S), :] = cells[g * S : g * S + S]
        return 0

    lax.fori_loop(0, mid_ref.shape[0], middle, 0, unroll=4)
    edge = 0
    for level in range(3):
        rate = 2**level
        edge += rate
        taps = taps_of(w_ref, level, half)

        def row(i, _, taps=taps, rate=rate, edge=edge, level=level):
            i = i + edge
            out = [convolved(bufs[level], width, taps, i, c, rate) for c in OUTER[level]]
            for c, v in zip(OUTER[level], out):
                bufs[level + 1][pl.ds(i * width + c, S), :] = v.astype(F32)
            return 0

        lax.fori_loop(0, rows0 - 2 * edge, row, 0, unroll=U_OUT)

        def clear(i, level=level):
            for c in range(0, width, S):
                bufs[level + 1][pl.ds(i * width + c, S), :] = jnp.zeros((S, 128), F32)

        clear_outside(first, rows0, lats, clear)

    taps = taps_of(w_ref, 3, half)
    other = (1 - half) * rows
    for ref, base in ((near_ref, other), (far_ref, other + rows // 2), (keep_ref, half * rows)):

        def last(i, _, ref=ref, base=base):
            row = base + REACH + i
            out = [
                done_ref[base + i] if q == MIDDLE[0] else convolved(bufs[3], width, taps, row, HALO + q * S, 8)
                for q in range(cols // S)
                if q not in MIDDLE[1:]
            ]
            ref[i] = jnp.concatenate(out, 0)
            return 0

        lax.fori_loop(0, ref.shape[0], last, 0, unroll=U_LAST)


def outer_levels(left, right, edge, mid, done, taps, lats, rows, cols):
    rows0 = edge.shape[1]
    shapes = [jax.ShapeDtypeStruct((r, cols, 128), BF) for r in (rows, rows // 2, rows // 2)]
    return pl.pallas_call(
        functools.partial(outer_kernel, lats),
        out_shape=shapes,
        in_specs=[VMEM] * 6,
        out_specs=[VMEM] * 3,
        scratch_shapes=[pltpu.VMEM((rows0 * (cols + 2 * HALO), 128), F32)] * 4,
        compiler_params=pltpu.CompilerParams(vmem_limit_bytes=LIMIT),
        cost_estimate=pl.CostEstimate(flops=40000000, bytes_accessed=4000000, transcendentals=500000),
        name="outer_levels",
    )(left, right, edge, mid, done, taps)


def feed(part, keep_ref, got_ref, gu_ref, down_ref):
    rows, cols, _ = got_ref.shape
    half = lax.axis_index("half")
    keep = keep_ref[part * rows : part * rows + rows].reshape(rows * cols, 128)
    got = got_ref[...].reshape(rows * cols, 128)
    state = jnp.concatenate([jnp.where(half == 0, keep, got), jnp.where(half == 0, got, keep)], -1).astype(F32)
    both = mm(norm(state), gu_ref[...])
    units = gu_ref.shape[1] // 2
    gate, up = both[:, :units], both[:, units:]
    hidden = (gate / (1.0 + jnp.exp(-gate)) * up).astype(BF)
    out = (state + mm(hidden, down_ref[...])).astype(BF)
    return out.reshape(rows, cols, 256)


def first_kernel(keep_ref, got_ref, gu_ref, down_ref, o_ref):
    o_ref[...] = feed(0, keep_ref, got_ref, gu_ref, down_ref)


def second_kernel(keep_ref, got_ref, gu_ref, down_ref, before_ref, o_ref, o_s, sems):
    rows = got_ref.shape[0]
    first = pltpu.make_async_copy(before_ref, o_ref.at[pl.ds(0, rows)], sems.at[0])
    first.start()
    o_s[...] = feed(1, keep_ref, got_ref, gu_ref, down_ref)
    second = pltpu.make_async_copy(o_s, o_ref.at[pl.ds(rows, rows)], sems.at[1])
    second.start()
    first.wait()
    second.wait()


def feed_forward(keep, got, gate_up, down, before=None):
    shape = got.shape[:2] + (256,)
    more = [] if before is None else [before]
    last = bool(more)
    return pl.pallas_call(
        second_kernel if last else first_kernel,
        out_shape=jax.ShapeDtypeStruct(keep.shape[:2] + (256,) if last else shape, BF),
        in_specs=[VMEM] * (4 + len(more)),
        out_specs=pl.BlockSpec(memory_space=pl.ANY) if last else VMEM,
        scratch_shapes=[pltpu.VMEM(shape, BF), pltpu.SemaphoreType.DMA((2,))] if last else [],
        compiler_params=pltpu.CompilerParams(vmem_limit_bytes=LIMIT),
        cost_estimate=pl.CostEstimate(flops=700000000, bytes_accessed=2000000, transcendentals=500000),
        name="feed_forward",
    )(keep, got, gate_up, down, *more)


def selection(lats, rows):
    blocks = lats // rows
    span = 2 * rows + 2 * REACH
    pitch = -(-span // 16) * 16
    pick = np.zeros((blocks // 2 * pitch, lats), np.float32)
    for p in range(blocks // 2):
        for r in range(span):
            lat = 2 * p * rows - REACH + r
            if 0 <= lat < lats:
                at = lat // rows
                pick[p * pitch + r, (lat % rows) * blocks + at % 2 * (blocks // 2) + at // 2] = 1
    return pick.astype(BF)


def on_device(
    grid_state,
    row_query,
    row_keyval,
    row_output,
    column_query,
    column_keyval,
    column_output,
    conv_kernel,
    gate_up,
    down_proj,
):
    rows, cols, width = grid_state.shape
    n = lax.axis_size("lon")
    m = 2 * lax.axis_size("block")
    lat = ("half", "block")
    lons = cols // m
    padded = jnp.pad(grid_state, ((0, n - rows), (0, 0), (0, 0)))
    lines = lax.all_to_all(padded, "lon", 0, 0, tiled=True).reshape(n * cols, width)
    after_rows = row_attention(lines, row_query, row_keyval, row_output)
    moved = lax.all_to_all(after_rows.reshape(n * m, 2 * lons, 128), ("lon",) + lat, 0, 0, tiled=True)
    moved = moved.reshape(-1, 128)
    pick = jnp.asarray(selection(rows * m, rows))
    span = 2 * rows + 2 * REACH
    sent = column_attention(moved, column_query, column_keyval, column_output, pick, lons, span, m)
    own = lax.all_to_all(sent, lat, 0, 0, tiled=True)
    k = HALO // lons
    left = lax.ppermute(own[m - k :], "lon", [(i, (i + 1) % n) for i in range(n)])
    right = lax.ppermute(own[:k], "lon", [((i + 1) % n, i) for i in range(n)])
    taps = jnp.swapaxes(conv_kernel, 0, 1)
    edge, mid, done = inner_levels(own, taps, rows * m, rows)
    keep, near, far = outer_levels(left, right, edge, mid, done, taps, rows * m, rows, cols)
    swap = [(0, 1), (1, 0)]
    got = [lax.ppermute(part, "half", swap) for part in (near, far)]
    out = feed_forward(keep, got[0], gate_up, down_proj)
    return feed_forward(keep, got[1], gate_up, down_proj, out)


def solution(mesh):
    n, m = mesh.devices.shape
    pairs = jax.sharding.Mesh(mesh.devices.reshape(n, m // 2, 2), ("lon", "block", "half"))
    cells = P(("block", "half"), "lon", None)
    return jax.shard_map(
        on_device,
        mesh=pairs,
        in_specs=(cells, P(), P(), P(), P(), P(), P(), P(), P(), P()),
        out_specs=cells,
        check_vma=False,
    )
```
